128 devices in a mesh: dp: 4 (over x_hi, core), fsdp: 32 (over z, y, x_lo).
Axes of the slice: x: 4 (x_hi: 2, x_lo: 2; x = x_hi * 2 + x_lo), y: 4, z: 4, core: 2. Of those that a mesh axis runs over, the one named last changes fastest.
Arguments:
- xbc: bfloat16 [16384, 10240], P(('dp', 'fsdp')), may hold values from -6 to 6
- zgate: bfloat16 [16384, 8192], P(('dp', 'fsdp')), may hold values from -6 to 6
- dt_raw: float32 [16384, 128], P(('dp', 'fsdp')), may hold values from -5 to 5
- prompt_states: bfloat16 [32, 128, 64, 128], P(None, ('dp', 'fsdp')), may hold values from -3 to 3
- conv_tails: bfloat16 [32, 3, 10240], P(None, None, ('dp', 'fsdp')), may hold values from -6 to 6
- resp_prompt: int32 [512], replicated, may hold values from 0 to 31, as said below
- resp_lengths: int32 [128, 4], P(('dp', 'fsdp')), may hold values from 1 to 80, 128 in all within a row
- rewards: float32 [512], replicated, may hold values from -4 to 4
- upstream: bfloat16 [16384, 8192], P(('dp', 'fsdp')), may hold values from -6 to 6
- conv_weight: float32 [4, 10240], P(None, 'fsdp'), may hold values from -3 to 3
- conv_bias: float32 [10240], P('fsdp'), may hold values from -3 to 3
- dt_bias: float32 [128], P('fsdp'), may hold values from -3 to -1
- a_log: float32 [128], P('fsdp'), may hold values from -5 to -0.7
- d_skip: float32 [128], P('fsdp'), may hold values from 0.5 to 1.5
- norm_gain: float32 [8192], P('fsdp'), may hold values from 0.5 to 1.5
Outputs:
- grad_xbc: bfloat16 [16384, 10240], P(('dp', 'fsdp'))
- grad_zgate: bfloat16 [16384, 8192], P(('dp', 'fsdp'))
- grad_dt_raw: float32 [16384, 128], P(('dp', 'fsdp'))
- grad_prompt_states: float32 [32, 128, 64, 128], P(None, ('dp', 'fsdp'))
- grad_conv_tails: float32 [32, 3, 10240], P(None, None, ('dp', 'fsdp'))
- grad_conv_weight: float32 [4, 10240], P(None, 'fsdp')
- grad_conv_bias: float32 [10240], P('fsdp')
- grad_dt_bias: float32 [128], P('fsdp')
- grad_a_log: float32 [128], P('fsdp')
- grad_d_skip: float32 [128], P('fsdp')
- grad_norm_gain: float32 [8192], P('fsdp')
The draws below stay inside these ranges and needn't reach their ends.
Inputs may be any that keep to these rules, and one draw needn't show every extreme that they name: `resp_prompt`: each of the 32 prompts is named by exactly 16 responses. `resp_lengths`: the 4 lengths of one device sum to 128.
All inputs are finite; a program needn't handle non-finite values.
Results may differ from the reference program's by a relative error of at most 0.0011.
Values may be sent and summed in bfloat16 or wider, within the bound.
No kernel may reach another device: no remote copies, remote signals or barrier semaphores. Data moves between devices by JAX's collectives and lax.ppermute only.
A program may use at most 192 MiB of HBM per device.

```python
import math
import jax
import jax.numpy as jnp
import numpy as np
from jax import lax

TOK_DEV = 128
DOCS_DEV = 4
GROUP = 16
H = 128
P_SIZE = 64
N = 128
G = 8
GS = 2048
DI = 8192
CONV = 10240
LMAX = 80
HOLDERS = 128
TOKENS = 16384
RESPONSES = 512
PROMPTS = 32
N_DP = 4
N_FSDP = 32


def draw_resp_prompt(key, part):
    key = jax.random.fold_in(key, 7)
    return (jax.random.permutation(key, RESPONSES) // GROUP).astype(jnp.int32)


def shard_levels(own_key, dims, pieces, least, largest):
    level, own = 1.0, jax.random.fold_in(own_key, 6)
    for dim, blocks in pieces:
        heights = jnp.exp(jax.random.uniform(jax.random.fold_in(own, dim), (blocks,), jnp.float32, least / len(pieces), largest / len(pieces)))
        level = level * jnp.repeat(heights, dims[dim] // blocks).reshape([-1 if axis == dim else 1 for axis in range(len(dims))])
    return level


def split_up(count, total, most, slope):
    loads = [(1 << 20) // math.isqrt(grade ** slope) + 1 for grade in range(2, count + 1)]
    spare, given = total - most - (count - 1), [1] * (count - 1)
    while spare > 0:
        free = [i for i in range(count - 1) if given[i] < most]
        whole, left = sum([loads[i] for i in free]), spare
        for i in free:
            more = min(most - given[i], max(1, left * loads[i] // whole), spare)
            given[i] = given[i] + more
            spare = spare - more
    return np.array([most] + given)


def uneven(rng, count, total, reach, slope):
    if count == 2:
        one = jax.random.randint(rng, (), max(1, total - reach), min(reach, total - 1) + 1)
        return jnp.stack([one, total - one])
    tallies = jnp.asarray(split_up(count, total, reach, slope), jnp.int32)
    couples = (count - 1) // 2
    donor, taker = tallies[1:1 + 2 * couples:2], tallies[2:2 + 2 * couples:2]
    room = jnp.minimum(donor - 1, reach - taker)
    passed = jax.random.randint(jax.random.fold_in(rng, 1), (couples,), 0, 1 << 20) % (room + 1)
    tallies = tallies.at[1:1 + 2 * couples:2].set(donor - passed).at[2:2 + 2 * couples:2].set(taker + passed)
    return tallies[jax.random.permutation(jax.random.fold_in(rng, 2), count)]


def bell_draw(key, dims, width, most, shards=(), kind=jnp.bfloat16):
    factor_of = shard_levels(key, dims, shards, -0.22, 0.18) if shards else 1.0
    result = jax.random.normal(key, dims, jnp.float32) * width * factor_of
    return jnp.minimum(jnp.maximum(result, -most), most).astype(kind)


def setup_inputs(seed: int = 0) -> dict:
    key_of = jax.random.split(jax.random.key(seed), 16)
    xbc = bell_draw(key_of[0], (TOKENS, CONV), 1.0, 6.0, ((0, 128),))
    zgate = bell_draw(key_of[1], (TOKENS, DI), 1.0, 6.0, ((0, 128),))
    dt_raw = bell_draw(key_of[2], (TOKENS, H), 1.0, 5.0, ((0, 128),), jnp.float32)
    prompt_states = bell_draw(key_of[3], (PROMPTS, H, P_SIZE, N), 0.5, 3.0, ((1, 128),))
    conv_tails = bell_draw(key_of[4], (PROMPTS, 3, CONV), 1.0, 6.0, ((2, 128),))
    resp_prompt = draw_resp_prompt(jax.random.fold_in(key_of[15], 71), 0)
    resp_lengths = jax.vmap(lambda own: uneven(own, DOCS_DEV, TOK_DEV, LMAX, 2))(jax.random.split(key_of[6], HOLDERS)).reshape((HOLDERS, DOCS_DEV)).astype(jnp.int32)
    rewards = bell_draw(key_of[7], (RESPONSES,), 1.0, 4.0, (), jnp.float32)
    upstream = bell_draw(key_of[8], (TOKENS, DI), 1.0, 6.0, ((0, 128),))
    conv_weight = bell_draw(key_of[9], (4, CONV), 4 ** -0.5, 3.0, ((1, 32),), jnp.float32)
    conv_bias = bell_draw(key_of[10], (CONV,), 0.5, 3.0, ((0, 32),), jnp.float32)
    dt_bias = jnp.clip(-3.0 + 2.0 * jax.random.uniform(key_of[11], (H,), jnp.float32) ** shard_levels(key_of[11], (H,), ((0, 32),), -0.2, 0.2), -3.0, -1.0)
    a_log = jnp.clip(-5.0 + 4.3 * jax.random.uniform(key_of[12], (H,), jnp.float32) ** shard_levels(key_of[12], (H,), ((0, 32),), -0.2, 0.2), -5.0, -0.7)
    d_skip = jnp.clip(0.5 + 1.0 * jax.random.uniform(key_of[13], (H,), jnp.float32) ** shard_levels(key_of[13], (H,), ((0, 32),), -0.2, 0.2), 0.5, 1.5)
    norm_gain = jnp.clip(1.0 + 0.1 * jax.random.normal(key_of[14], (DI,), jnp.float32), 0.5, 1.5)
    return {"xbc": xbc, "zgate": zgate, "dt_raw": dt_raw, "prompt_states": prompt_states, "conv_tails": conv_tails, "resp_prompt": resp_prompt, "resp_lengths": resp_lengths, "rewards": rewards, "upstream": upstream, "conv_weight": conv_weight, "conv_bias": conv_bias, "dt_bias": dt_bias, "a_log": a_log, "d_skip": d_skip, "norm_gain": norm_gain}


def advantages(rewards, resp_prompt, prompt_count):
    member = (resp_prompt[:, None] == jnp.arange(prompt_count, dtype=jnp.int32)[None, :]).astype(jnp.float32)
    group_mean = jnp.dot(rewards, member, precision=lax.Precision.HIGHEST) / GROUP
    centred = rewards - jnp.dot(member, group_mean, precision=lax.Precision.HIGHEST)
    spread = jnp.sqrt(jnp.dot(centred * centred, member, precision=lax.Precision.HIGHEST) / GROUP)
    return centred / jnp.dot(member, jnp.maximum(spread, 0.8), precision=lax.Precision.HIGHEST)

def token_layout(lengths, row_count):
    places = jnp.arange(row_count, dtype=jnp.int32)
    doc_ends = jnp.cumsum(lengths).astype(jnp.int32)
    doc_starts = (doc_ends - lengths).astype(jnp.int32)
    member = (places[:, None] >= doc_starts[None, :]) & (places[:, None] < doc_ends[None, :])
    start_tok = lax.optimization_barrier(jnp.sum(jnp.where(member, doc_starts[None, :], 0), axis=1)).astype(jnp.int32)
    return (member, start_tok, (places - start_tok).astype(jnp.int32))

def conv_branch(signal, tail_rows, conv_w, conv_b, member, offset):
    row_count = signal.shape[0]
    summed = conv_w[3][None, :] * signal
    for delay_step in (1, 2, 3):
        lagged = jnp.concatenate([jnp.zeros((delay_step, signal.shape[1]), jnp.float32), signal[:-delay_step]], axis=0)
        summed = summed + jnp.where((offset >= delay_step)[:, None], lagged, 0.0) * conv_w[3 - delay_step][None, :]
    tail_a = tail_rows[:, 0, :]
    tail_b = tail_rows[:, 1, :]
    tail_c = tail_rows[:, 2, :]
    w_zero = conv_w[0][None, :]
    w_one = conv_w[1][None, :]
    w_two = conv_w[2][None, :]
    lead_in = jnp.stack([w_two * tail_c + w_one * tail_b + w_zero * tail_a, w_one * tail_c + w_zero * tail_b, w_zero * tail_c], axis=1)
    select = (member[:, :, None] & (offset[:, None, None] == jnp.arange(3, dtype=jnp.int32)[None, None, :])).astype(jnp.float32)
    summed = summed + jnp.dot(select.reshape(row_count, -1), lead_in.reshape(-1, signal.shape[1]), precision=lax.Precision.HIGHEST)
    return jax.nn.silu(summed + conv_b[None, :])

def mixer_forward(signal, gate_in, dt_in, states, tail_rows, params, member, start_tok, offset):
    conv_w, conv_b, bias_dt, log_rate, skip_all, gain = params
    row_count = signal.shape[0]
    doc_count = states.shape[0]
    inner = H * P_SIZE
    per_group = H // G
    conv_out = conv_branch(signal, tail_rows, conv_w, conv_b, member, offset)
    x_heads = conv_out[:, :inner].reshape(row_count, G, per_group, P_SIZE).transpose(1, 0, 2, 3)
    b_all = conv_out[:, inner:inner + G * N].reshape(row_count, G, N).transpose(1, 0, 2)
    c_all = conv_out[:, inner + G * N:].reshape(row_count, G, N).transpose(1, 0, 2)
    step_size = jax.nn.softplus(dt_in + bias_dt[None, :])
    decay_log = -step_size * jnp.exp(log_rate)[None, :]
    cum_log = jnp.cumsum(decay_log, axis=0)
    base_log = jnp.take(cum_log - decay_log, start_tok, axis=0)
    rel_log = cum_log - base_log
    places = jnp.arange(row_count, dtype=jnp.int32)
    causal = (start_tok[:, None] == start_tok[None, :]) & (places[:, None] >= places[None, :])
    member_f = member.astype(jnp.float32)

    def by_group(table):
        return table.reshape(row_count, G, per_group).transpose(1, 0, 2)
    start_all = states.reshape(doc_count, G, per_group, P_SIZE, N).transpose(1, 0, 2, 3, 4)

    def group_mix(items):
        c_rows, b_rows, x_rows, steps_g, cum_g, rel_g, start_state, skip_gain = items
        scores = jnp.dot(c_rows, b_rows.T, precision=lax.Precision.HIGHEST)
        log_gaps = cum_g.T[:, :, None] - cum_g.T[:, None, :]
        decays = jnp.exp(jnp.where(causal[None], log_gaps, -jnp.inf))
        weights = decays * scores[None] * steps_g.T[:, None, :]
        within = jnp.einsum('kts,skp->tkp', weights, x_rows, precision=lax.Precision.HIGHEST)
        c_masked = member_f[:, :, None] * c_rows[:, None, :]
        carried = jnp.einsum('tdn,dkpn->tkp', c_masked, start_state, precision=lax.Precision.HIGHEST)
        carried = carried * jnp.exp(rel_g)[:, :, None]
        return within + carried + skip_gain[None, :, None] * x_rows
    mixed_out = lax.map(jax.checkpoint(group_mix), (c_all, b_all, x_heads, by_group(step_size), by_group(cum_log), by_group(rel_log), start_all, skip_all.reshape(G, per_group)))
    mixed_out = mixed_out.transpose(1, 0, 2, 3).reshape(row_count, inner)
    gated_out = mixed_out * jax.nn.silu(gate_in)
    grouped = gated_out.reshape(row_count, inner // GS, GS)
    inv_rms = lax.rsqrt(lax.optimization_barrier(jnp.mean(grouped * grouped, axis=-1, keepdims=True)) + 1e-05)
    return (grouped * inv_rms).reshape(row_count, inner) * gain[None, :]

def local_grads(signal_in, gate_in, dt_in, states, tail_rows, params, lengths, upstream, doc_weight):
    member, start_tok, offset = token_layout(lengths, signal_in.shape[0])
    tok_weight = lax.optimization_barrier(jnp.sum(jnp.where(member, doc_weight[None, :], 0.0), axis=1))

    def forward(signal, gate_vals, dt_vals, state_vals, tail_vals, weight_vals):
        return mixer_forward(signal, gate_vals, dt_vals, state_vals, tail_vals, weight_vals, member, start_tok, offset)
    primal_out, pullback = jax.vjp(forward, signal_in.astype(jnp.float32), gate_in.astype(jnp.float32), dt_in, states.astype(jnp.float32), tail_rows.astype(jnp.float32), params)
    return pullback(upstream.astype(jnp.float32) * tok_weight[:, None])

def reference(xbc, zgate, dt_raw, prompt_states, conv_tails, resp_prompt, resp_lengths, rewards, upstream, conv_weight, conv_bias, dt_bias, a_log, d_skip, norm_gain):
    params = (conv_weight, conv_bias, dt_bias, a_log, d_skip, norm_gain)
    advantage = advantages(rewards, resp_prompt, PROMPTS)

    def device_step(running, holder):
        first_row = (holder * TOK_DEV).astype(jnp.int32)
        first_doc = (holder * DOCS_DEV).astype(jnp.int32)
        prompt_ids = lax.dynamic_slice_in_dim(resp_prompt, first_doc, DOCS_DEV)
        lengths = resp_lengths[holder]
        doc_weight = lax.dynamic_slice_in_dim(advantage, first_doc, DOCS_DEV) * (TOK_DEV / (DOCS_DEV * lengths.astype(jnp.float32)))
        gradients = local_grads(lax.dynamic_slice_in_dim(xbc, first_row, TOK_DEV), lax.dynamic_slice_in_dim(zgate, first_row, TOK_DEV), lax.dynamic_slice_in_dim(dt_raw, first_row, TOK_DEV), prompt_states[prompt_ids], conv_tails[prompt_ids], params, lengths, lax.dynamic_slice_in_dim(upstream, first_row, TOK_DEV), doc_weight)
        grad_x, grad_z, grad_dt, grad_state, grad_tail, grad_param = gradients
        state_sum, tail_sum, param_sum = running
        state_sum = state_sum.at[prompt_ids].add(grad_state)
        tail_sum = tail_sum.at[prompt_ids].add(grad_tail)
        param_sum = jax.tree.map(jnp.add, param_sum, grad_param)
        return ((state_sum, tail_sum, param_sum), (grad_x.astype(jnp.bfloat16), grad_z.astype(jnp.bfloat16), grad_dt))
    param_zero = tuple((jnp.zeros(weight.shape, jnp.float32) for weight in params))
    start_carry = (jnp.zeros(prompt_states.shape, jnp.float32), jnp.zeros(conv_tails.shape, jnp.float32), param_zero)
    final_carry, stacked = lax.scan(device_step, start_carry, jnp.arange(N_DP * N_FSDP, dtype=jnp.int32))
    state_sum, tail_sum, param_sum = final_carry
    grad_x, grad_z, grad_dt = stacked
    return (grad_x.reshape(TOKENS, CONV), grad_z.reshape(TOKENS, DI), grad_dt.reshape(TOKENS, H), state_sum, tail_sum, param_sum[0], param_sum[1], param_sum[2], param_sum[3], param_sum[4], param_sum[5])
```

```python
import functools

import jax
import jax.numpy as jnp
from jax import lax
from jax.experimental import pallas as pl
from jax.experimental.pallas import tpu as pltpu
from jax.sharding import PartitionSpec as P

GROUP = 16
T = 128
DOCS = 4
H = 128
P_SIZE = 64
N = 128
G = 8
HG = H // G
GC = HG * P_SIZE
GS = 2048
DI = 8192
CONV = 10240
PROMPTS = 32
SRC = 8

F32 = jnp.float32
BF16 = jnp.bfloat16
NN = (((1,), (0,)), ((), ()))
NT = (((1,), (1,)), ((), ()))
TN = (((0,), (0,)), ((), ()))
AXES = ("dp", "fsdp")


def mm(a, b, dims=NN):
    return lax.dot_general(a, b, dims, preferred_element_type=F32)


def split(a):
    hi = a.astype(BF16)
    return hi, (a - hi.astype(F32)).astype(BF16)


def mm3(a, b, dims=NN):
    ah, al = split(a)
    bh, bl = split(b)
    return mm(ah, bh, dims) + (mm(ah, bl, dims) + mm(al, bh, dims))


def cat(parts, axis):
    return jnp.concatenate(parts, axis=axis)


def sigmoid(a):
    return 1.0 / (1.0 + jnp.exp(-a))


def lanes(rows=T):
    return lax.broadcasted_iota(jnp.int32, (rows, 128), 1)


def head_sum_matrix(first):
    row = lax.broadcasted_iota(jnp.int32, (128, 128), 0)
    col = lax.broadcasted_iota(jnp.int32, (128, 128), 1)
    return (col == first + row // P_SIZE).astype(BF16)


def lagged(u, tails, sel, off):
    led = mm(sel, tails.astype(BF16))
    out = []
    for k in (1, 2, 3):
        back = jnp.where(off >= k, pltpu.roll(u, k, axis=0), 0.0)
        out.append(back + led[(k - 1) * T : k * T])
    return out


def conv_forward(raw, tails, w, bias, sel, off):
    u = raw.astype(F32)
    l1, l2, l3 = lagged(u, tails, sel, off)
    a = bias + w[3:4] * u + w[2:3] * l1 + w[1:2] * l2 + w[0:1] * l3
    sig = sigmoid(a)
    return a * sig, sig * (1.0 + a * (1.0 - sig))


def conv_backward(dout, sp, raw, tails, w, sel, sel_t, off):
    u = raw.astype(F32)
    l1, l2, l3 = lagged(u, tails, sel, off)
    da = dout * sp
    width = da.shape[1]
    sums = [jnp.sum(da * f, axis=0, keepdims=True) for f in (l3, l2, l1, u)]
    sums.append(jnp.sum(da, axis=0, keepdims=True))
    sums.append(jnp.zeros((3, width), F32))
    du = w[3:4] * da
    parts = []
    for k in (1, 2, 3):
        term = w[3 - k : 4 - k] * da
        parts.append(term)
        du = du + pltpu.roll(jnp.where(off >= k, term, 0.0), T - k, axis=0)
    hi, lo = split(cat(parts, 0))
    return du, cat(sums, 0), mm(sel_t, hi) + mm(sel_t, lo)


def local_kernel(
    xr, br, cr, tx, tb, tc, wx, wb, wc, bx, bb, bc, off_ref, sel_ref,
    caus_ref, rel_ref, relt_ref, stept_ref, dsk_ref,
    x_o, b_o, c_o, spx_o, spb_o, spc_o, m0_o, lw_o, exr_o, cq_o, sc_o, score_o,
):
    off = off_ref[...]
    sel = sel_ref[...]
    b, spb = conv_forward(br[...], tb[...], wb[...], bb[...], sel, off)
    c, spc = conv_forward(cr[...], tc[...], wc[...], bc[...], sel, off)
    b_o[...] = b
    c_o[...] = c
    spb_o[...] = spb
    spc_o[...] = spc
    scores = mm3(c, b, NT)
    score_o[0] = scores
    ceil = jnp.maximum(jnp.max(jnp.abs(c), axis=1, keepdims=True), 1e-30)
    cq = jnp.round(c * (32767.0 / ceil)).astype(jnp.int32).astype(jnp.int16)
    for h in range(HG):
        cq_o[h] = cq
    ceil_t = jnp.max(jnp.abs(c.T), axis=0, keepdims=True)
    sc_o[0] = jnp.maximum(ceil_t, 1e-30) * (1.0 / 32767.0)
    caus = caus_ref[...] > 0.0
    first = lanes() < P_SIZE
    for i in range(HG // 2):
        at = slice(128 * i, 128 * (i + 1))
        x, spx = conv_forward(xr[:, at], tx[:, at], wx[:, at], bx[:, at], sel, off)
        x_o[:, at] = x
        spx_o[:, at] = spx
        cols, weights = [], []
        for j in (2 * i, 2 * i + 1):
            col = jnp.broadcast_to(rel_ref[0, :, j : j + 1], (T, T))
            gap = jnp.where(caus, col - relt_ref[j : j + 1, :], -1e30)
            lw = jnp.exp(gap) * stept_ref[j : j + 1, :]
            lw_o[j] = lw
            cols.append(col)
            weights.append(lw * scores)
        exr_o[:, at] = jnp.exp(jnp.where(first, cols[0], cols[1]))
        wide = cat([jnp.where(first, x, 0.0), jnp.where(first, 0.0, x)], 0)
        m0_o[:, at] = mm3(cat(weights, 1), wide) + dsk_ref[:, at] * x


def norm_kernel(
    st_ref, c_ref, m0_ref, exr_ref, z_ref, up_ref, gain_ref, tokw_ref, memb_ref, sc_ref,
    dz_o, dm_o, q_o, s_o, dg_o, rs_o,
    mix_s,
):
    memb = memb_ref[...]
    tokw = tokw_ref[...]
    for gg in range(2):
        cg = c_ref[:, 128 * gg : 128 * (gg + 1)]
        hi, lo = split(cat([cg * memb[:, d : d + 1] for d in range(DOCS)], 1))
        rhs = cat(
            [st_ref[HG * gg : HG * (gg + 1), d].reshape(GC, N) for d in range(DOCS)], 1
        )
        both = mm(cat([hi, lo], 0), rhs, NT)
        at = slice(GC * gg, GC * (gg + 1))
        mix_s[:, at] = m0_ref[:, at] + (both[:T] + both[T:]) * exr_ref[:, at]
    squares = jnp.zeros((T, 128), F32)
    crossed = jnp.zeros((T, 128), F32)
    for i in range(GS // 128):
        at = slice(128 * i, 128 * (i + 1))
        z = z_ref[:, at].astype(F32)
        v = mix_s[:, at] * (z * sigmoid(z))
        dn = up_ref[:, at].astype(F32) * tokw * gain_ref[:, at]
        squares = squares + v * v
        crossed = crossed + dn * v
    r = lax.rsqrt(jnp.sum(squares, axis=1, keepdims=True) * (1.0 / GS) + 1e-05)
    k = r * r * r * (jnp.sum(crossed, axis=1, keepdims=True) * (1.0 / GS))
    r = jnp.broadcast_to(r, (T, 128))
    k = jnp.broadcast_to(k, (T, 128))
    rs = jnp.zeros((2 * T, 128), F32)
    for i in range(GS // 128):
        at = slice(128 * i, 128 * (i + 1))
        z = z_ref[:, at].astype(F32)
        sig = sigmoid(z)
        sz = z * sig
        mixed = mix_s[:, at]
        v = mixed * sz
        go = up_ref[:, at].astype(F32) * tokw
        dg_o[:, at] = jnp.sum(go * v * r, axis=0, keepdims=True)
        dv = r * (go * gain_ref[:, at]) - v * k
        dm = dv * sz
        dm_o[:, at] = dm
        dz_o[:, at] = (dv * mixed * (sig * (1.0 + z * (1.0 - sig)))).astype(BF16)
        hi, lo = split(dm * mixed)
        rs = rs + mm(cat([hi, lo], 0), head_sum_matrix(2 * i))
        turned = (dm * exr_ref[:, at]).T
        for j in range(2):
            h = 2 * i + j
            e = turned[P_SIZE * j : P_SIZE * (j + 1)]
            top = jnp.maximum(jnp.max(jnp.abs(e), axis=0, keepdims=True), 1e-30)
            q_o[h] = jnp.round(e * (32767.0 / top)).astype(jnp.int32).astype(jnp.int16)
            s_o[h : h + 1, :] = top * (1.0 / 32767.0) * sc_ref[h // HG]
    rs_o[0] = rs[:T] + rs[T:]


def back_kernel(
    st_ref, dm_ref, exr_ref, lw_ref, score_ref, x_ref, b_ref, c_ref,
    spx, spb, spc, xr, br, cr, tx, tb, tc, wx, wb, wc, off_ref, sel_ref, selt_ref,
    memb_ref, dsk_ref,
    gx_o, gb_o, gc_o, px_o, pb_o, pc_o, ttx_o, ttb_o, ttc_o, rx_o, cq_o,
):
    off = off_ref[...]
    sel = sel_ref[...]
    sel_t = selt_ref[...]
    memb = memb_ref[...]
    b = b_ref[...]
    c = c_ref[...]
    scores = score_ref[0]
    hi, lo = split(dm_ref[...] * exr_ref[...])
    rhs = cat([st_ref[:, d].reshape(GC, N) for d in range(DOCS)], 1)
    both = mm(cat([hi, lo], 0), rhs)
    both = both[:T] + both[T:]
    dc = jnp.zeros((T, N), F32)
    for d in range(DOCS):
        dc = dc + both[:, N * d : N * (d + 1)] * memb[:, d : d + 1]
    first = lanes() < P_SIZE
    dscores = jnp.zeros((T, T), F32)
    rx = jnp.zeros((2 * T, 128), F32)
    for i in range(HG // 2):
        at = slice(128 * i, 128 * (i + 1))
        dm = dm_ref[:, at]
        x = x_ref[:, at]
        wide = cat([jnp.where(first, dm, 0.0), jnp.where(first, 0.0, dm)], 0)
        dweights = mm3(wide, x, NT)
        weights = []
        for j in range(2):
            lw = lw_ref[2 * i + j]
            g1 = dweights[T * j : T * (j + 1)] * lw
            dscores = dscores + g1
            cq_o[2 * i + j : 2 * i + j + 1, :] = jnp.sum(g1 * scores, axis=0, keepdims=True)
            weights.append(lw * scores)
        turned = wide_t(dm, first)
        dx = mm3(turned, cat(weights, 0)).T + dsk_ref[:, at] * dm
        hi, lo = split(dm * x)
        rx = rx + mm(cat([hi, lo], 0), head_sum_matrix(2 * i))
        du, sums, dt = conv_backward(
            dx, spx[:, at], xr[:, at], tx[:, at], wx[:, at], sel, sel_t, off
        )
        gx_o[:, at] = du.astype(BF16)
        px_o[:, at] = sums
        ttx_o[:, at] = dt
    rx_o[0] = rx[:T] + rx[T:]
    dc = dc + mm3(dscores, b)
    db = mm3(dscores.T, c)
    du, sums, dt = conv_backward(db, spb[...], br[...], tb[...], wb[...], sel, sel_t, off)
    gb_o[...] = du.astype(BF16)
    pb_o[...] = sums
    ttb_o[...] = dt
    du, sums, dt = conv_backward(dc, spc[...], cr[...], tc[...], wc[...], sel, sel_t, off)
    gc_o[...] = du.astype(BF16)
    pc_o[...] = sums
    ttc_o[...] = dt


def wide_t(dm, first):
    t = dm.T
    z = jnp.zeros((P_SIZE, T), F32)
    return cat([cat([t[:P_SIZE], z], 1), cat([z, t[P_SIZE:]], 1)], 0)


def state_kernel(prompt_ref, q_ref, c_ref, s_ref, mask_ref, out_ref):
    step = pl.program_id(0)

    @pl.when(step == 0)
    def _():
        out_ref[...] = jnp.zeros_like(out_ref)

    for i in range(SRC):
        q = q_ref[i].astype(jnp.int32).astype(F32) * s_ref[i : i + 1, :]
        hi, lo = split(q)
        ci = c_ref[i].astype(jnp.int32)
        low = ci & 255
        high = (ci - low).astype(F32).astype(BF16)
        low = low.astype(F32).astype(BF16)
        rhs = cat([high, high, low, low], 0)
        rows = []
        for d in range(DOCS):
            m = jnp.broadcast_to(mask_ref[i, d : d + 1, :], (P_SIZE, T)).astype(BF16)
            rows.append(cat([hi * m, lo * m] * 2, 1))
        got = mm(cat(rows, 0), rhs)
        for d in range(DOCS):
            p = prompt_ref[(step * SRC + i) * DOCS + d]
            out_ref[p] = out_ref[p] + got[P_SIZE * d : P_SIZE * (d + 1)]


def whole(shape):
    return pl.BlockSpec(shape, lambda g, *_: (0,) * len(shape))


def cols(rows, width, first=0):
    return pl.BlockSpec((rows, width), lambda g, *_: (0, first + g))


def lead(*shape):
    return pl.BlockSpec(shape, lambda g, *_: (g,) + (0,) * (len(shape) - 1))


def shape(dims, dtype=F32):
    return jax.ShapeDtypeStruct(dims, dtype)


def call(body, grid, in_specs, out_specs, out_shape, name, flops, nbytes, scratch=()):
    return pl.pallas_call(
        body,
        grid=grid,
        in_specs=in_specs,
        out_specs=out_specs,
        out_shape=out_shape,
        scratch_shapes=list(scratch),
        compiler_params=pltpu.CompilerParams(vmem_limit_bytes=56 * 1024 * 1024),
        cost_estimate=pl.CostEstimate(flops=flops, bytes_accessed=nbytes, transcendentals=0),
        name=name,
    )


def advantages(rewards, resp_prompt, prompt_count):
    member = (resp_prompt[:, None] == jnp.arange(prompt_count, dtype=jnp.int32)[None, :]).astype(F32)
    group_mean = jnp.dot(rewards, member, precision=lax.Precision.HIGHEST) / GROUP
    centred = rewards - jnp.dot(member, group_mean, precision=lax.Precision.HIGHEST)
    spread = jnp.sqrt(jnp.dot(centred * centred, member, precision=lax.Precision.HIGHEST) / GROUP)
    return centred / jnp.dot(member, jnp.maximum(spread, 0.8), precision=lax.Precision.HIGHEST)


def shards(
    xbc, zgate, dt_raw, prompt_states, conv_tails, resp_prompt, resp_lengths, rewards, upstream,
    conv_weight, conv_bias, dt_bias, a_log, d_skip, norm_gain,
):
    devices = lax.axis_size("dp") * lax.axis_size("fsdp")
    n_dp, n_fsdp = lax.axis_size("dp"), lax.axis_size("fsdp")
    dp = lax.axis_index("dp")
    holder = lax.axis_index(AXES)
    exchange = functools.partial(
        lax.all_to_all, axis_name=AXES, split_axis=0, concat_axis=0, tiled=True
    )

    weights = cat(
        [conv_weight.reshape(-1), conv_bias, dt_bias, a_log, d_skip, norm_gain], 0
    )
    count = weights.shape[0]
    weights = jnp.pad(weights, (0, 2048 - count))
    quarter = lax.dynamic_slice_in_dim(weights, dp * 512, 512)
    onehot = resp_prompt[:, None] == jnp.arange(PROMPTS, dtype=jnp.int32)[None, :]
    tails_sent = jnp.dot(
        onehot.astype(BF16), conv_tails.reshape(PROMPTS, 240), preferred_element_type=F32
    )
    lengths_f = jnp.broadcast_to(resp_lengths.astype(F32), (devices, DOCS))
    sent = cat(
        [
            tails_sent.reshape(devices, 960),
            lengths_f,
            jnp.zeros((devices, 60), F32),
            jnp.broadcast_to(quarter[None], (devices, 512)),
        ],
        1,
    )
    got = exchange(sent.reshape(devices, 12, 128)).reshape(devices, 1536)
    states = exchange(
        prompt_states[resp_prompt].reshape(devices, DOCS, P_SIZE, N)
    )

    tails = got[:, :960].reshape(devices, 12, 80).transpose(1, 0, 2).reshape(12, CONV)
    tails = jnp.pad(tails, ((0, 4), (0, 0)))
    all_lengths = got[:, 960:964].astype(jnp.int32)
    full = got[:, 1024:].reshape(n_dp, n_fsdp, 512).transpose(1, 0, 2).reshape(n_fsdp, 2048)
    conv_w = full[:, :1280].reshape(n_fsdp, 4, 320).transpose(1, 0, 2).reshape(4, CONV)
    conv_b = full[:, 1280:1600].reshape(1, CONV)
    bias_dt = full[:, 1600:1604].reshape(1, H)
    rate = jnp.exp(full[:, 1604:1608].reshape(1, H))
    skip = full[:, 1608:1612].reshape(1, H)
    gain = full[:, 1612:1868].reshape(1, DI)

    lengths = resp_lengths[0]
    places = jnp.arange(T, dtype=jnp.int32)
    ends = jnp.cumsum(lengths)
    starts = ends - lengths
    member = (places[:, None] >= starts[None, :]) & (places[:, None] < ends[None, :])
    start = jnp.sum(jnp.where(member, starts[None, :], 0), axis=1)
    offset = (places - start)[:, None]
    causal = ((start[:, None] == start[None, :]) & (places[:, None] >= places[None, :])).astype(F32)
    member_f = member.astype(F32)
    lag = jnp.arange(1, 4, dtype=jnp.int32)[:, None, None, None]
    row = jnp.arange(3, dtype=jnp.int32)[None, None, None, :]
    sel = member[None, :, :, None] & (offset[None, :, :, None] - lag + 3 == row)
    sel = jnp.pad(sel.reshape(3 * T, 12).astype(BF16), ((0, 0), (0, 4)))
    all_ends = jnp.cumsum(all_lengths, axis=1)
    all_starts = all_ends - all_lengths
    mask_rows = (
        (places[None, None, :] >= all_starts[:, :, None])
        & (places[None, None, :] < all_ends[:, :, None])
    ).astype(F32)
    advantage = advantages(rewards, resp_prompt, PROMPTS)
    doc_weight = lax.dynamic_slice_in_dim(advantage, holder * DOCS, DOCS) * (
        T / (DOCS * lengths.astype(F32))
    )
    tokw = jnp.sum(jnp.where(member, doc_weight[None, :], 0.0), axis=1)[:, None]

    raw_step = dt_raw + bias_dt
    step = jax.nn.softplus(raw_step)
    decay = -step * rate
    rel = jnp.dot(causal, decay, precision=lax.Precision.HIGHEST)
    rel_g = rel.reshape(T, G, HG).transpose(1, 0, 2)
    skip_wide = jnp.repeat(skip, P_SIZE, axis=1)

    conv_specs = [cols(T, GC), cols(T, N, 64), cols(T, N, 72)]
    tail_specs = [cols(16, GC), cols(16, N, 64), cols(16, N, 72)]
    tap_specs = [cols(4, GC), cols(4, N, 64), cols(4, N, 72)]
    bias_specs = [cols(1, GC), cols(1, N, 64), cols(1, N, 72)]
    x, b, c, spx, spb, spc, mixed0, lw, exr, cq, sc, scores = call(
        local_kernel,
        (G,),
        conv_specs + tail_specs + tap_specs + bias_specs
        + [whole((T, 1)), whole((3 * T, 16)), whole((T, T)), lead(1, T, HG), lead(HG, T), lead(HG, T),
           cols(1, GC)],
        [cols(T, GC), cols(T, N), cols(T, N), cols(T, GC), cols(T, N), cols(T, N), cols(T, GC),
         lead(HG, T, T), cols(T, GC), lead(HG, T, N), lead(1, 1, T), lead(1, T, T)],
        [shape((T, DI)), shape((T, G * N)), shape((T, G * N)), shape((T, DI)), shape((T, G * N)),
         shape((T, G * N)), shape((T, DI)), shape((H, T, T)), shape((T, DI)),
         shape((H, T, N), jnp.int16), shape((G, 1, T)), shape((G, T, T))],
        "local_forward", 2 * 10**9, 40 * 10**6,
    )(xbc, xbc, xbc, tails, tails, tails, conv_w, conv_w, conv_w, conv_b, conv_b, conv_b,
      offset, sel, causal, rel_g, rel.T, step.T, skip_wide)

    states, cq = lax.optimization_barrier((states, cq))
    got_c = exchange(cq)
    grad_z, dm, q, scale, d_gain, rs = call(
        norm_kernel,
        (4,),
        [lead(32, DOCS, P_SIZE, N), cols(T, 2 * N), cols(T, GS), cols(T, GS), cols(T, GS), cols(T, GS),
         cols(1, GS), whole((T, 1)), whole((T, DOCS)), lead(2, 1, T)],
        [cols(T, GS), cols(T, GS), lead(32, P_SIZE, T), lead(32, T), cols(1, GS), lead(1, T, 128)],
        [shape((T, DI), BF16), shape((T, DI)), shape((H, P_SIZE, T), jnp.int16), shape((H, T)),
         shape((1, DI)), shape((4, T, 128))],
        "norm_both_ways", 3 * 10**9, 35 * 10**6,
        [pltpu.VMEM((T, GS), F32)],
    )(states, c, mixed0, exr, zgate, upstream, gain, tokw, member_f, sc)
    got_q = exchange(q)
    got_s = exchange(scale.reshape(devices, 1, T)).reshape(devices, T)

    gx, gb, gc, px, pb, pc, ttx, ttb, ttc, rx, col_q = call(
        back_kernel,
        (G,),
        [lead(HG, DOCS, P_SIZE, N), cols(T, GC), cols(T, GC), lead(HG, T, T), lead(1, T, T),
         cols(T, GC), cols(T, N), cols(T, N), cols(T, GC), cols(T, N), cols(T, N)]
        + conv_specs + tail_specs + tap_specs
        + [whole((T, 1)), whole((3 * T, 16)), whole((16, 3 * T)), whole((T, DOCS)), cols(1, GC)],
        [cols(T, GC), cols(T, N), cols(T, N), cols(8, GC), cols(8, N), cols(8, N), cols(16, GC),
         cols(16, N), cols(16, N), lead(1, T, 128), lead(HG, T)],
        [shape((T, DI), BF16), shape((T, G * N), BF16), shape((T, G * N), BF16), shape((8, DI)),
         shape((8, G * N)), shape((8, G * N)), shape((16, DI)), shape((16, G * N)), shape((16, G * N)),
         shape((G, T, 128)), shape((H, T))],
        "local_backward", 4 * 10**9, 45 * 10**6,
    )(states, dm, exr, lw, scores, x, b, c, spx, spb, spc, xbc, xbc, xbc, tails, tails, tails,
      conv_w, conv_w, conv_w, offset, sel, sel.T, member_f, skip_wide)
    grad_x = cat([gx, gb, gc], 1)

    rs = rs[:, :, :32].transpose(1, 0, 2).reshape(T, H)
    rx = rx[:, :, :HG].transpose(1, 0, 2).reshape(T, H)
    col_q = col_q.T
    d_rel = rs - skip * rx - col_q
    d_decay = jnp.dot(causal.T, d_rel, precision=lax.Precision.HIGHEST)
    grad_dt = (col_q / step - rate * d_decay) * jax.nn.sigmoid(raw_step)
    d_alog = jnp.sum(decay * d_decay, axis=0)
    d_bias_dt = jnp.sum(grad_dt, axis=0)
    d_skip_out = jnp.sum(rx, axis=0)

    tails_back = cat([ttx, ttb, ttc], 1)[:12].reshape(12, devices, 80).transpose(1, 0, 2)
    taps = cat([px, pb, pc], 1)
    owned = cat(
        [
            taps[:4].reshape(4, n_fsdp, 320).transpose(1, 0, 2).reshape(n_fsdp, 1280),
            taps[4].reshape(n_fsdp, 320),
            d_bias_dt.reshape(n_fsdp, 4),
            d_alog.reshape(n_fsdp, 4),
            d_skip_out.reshape(n_fsdp, 4),
            d_gain.reshape(n_fsdp, 256),
        ],
        1,
    )
    back = cat(
        [
            tails_back.reshape(devices, 960),
            jnp.tile(owned, (n_dp, 1)),
            jnp.zeros((devices, 2944 - 960 - count), F32),
        ],
        1,
    )
    back = exchange(back.reshape(devices, 23, 128)).reshape(devices, 2944)

    grad_states = pl.pallas_call(
        state_kernel,
        grid_spec=pltpu.PrefetchScalarGridSpec(
            num_scalar_prefetch=1,
            grid=(devices // SRC,),
            in_specs=[lead(SRC, P_SIZE, T), lead(SRC, T, N), lead(SRC, T), lead(SRC, DOCS, T)],
            out_specs=whole((PROMPTS, P_SIZE, N)),
        ),
        out_shape=shape((PROMPTS, P_SIZE, N)),
        compiler_params=pltpu.CompilerParams(vmem_limit_bytes=56 * 1024 * 1024),
        cost_estimate=pl.CostEstimate(flops=4 * 10**9, bytes_accessed=8 * 10**6, transcendentals=0),
        name="state_gradients",
    )(resp_prompt, got_q, got_c, got_s, mask_rows)

    grad_tails = jnp.dot(
        onehot.astype(F32).T,
        back[:, :960].reshape(devices * DOCS, 240),
        precision=lax.Precision.HIGHEST,
    ).reshape(PROMPTS, 3, 80)
    total = jnp.sum(back[:, 960 : 960 + count], axis=0)
    return (
        grad_x,
        grad_z,
        grad_dt,
        grad_states.reshape(PROMPTS, 1, P_SIZE, N),
        grad_tails,
        total[:1280].reshape(4, 320),
        total[1280:1600],
        total[1600:1604],
        total[1604:1608],
        total[1608:1612],
        total[1612:1868],
    )


def solution(mesh):
    whole_axis = P(AXES, None)
    weight = P("fsdp")
    return jax.shard_map(
        shards,
        mesh=mesh,
        in_specs=(
            whole_axis, whole_axis, whole_axis, P(None, AXES, None, None), P(None, None, AXES),
            P(), whole_axis, P(), whole_axis, P(None, "fsdp"), weight, weight, weight, weight, weight,
        ),
        out_specs=(
            whole_axis, whole_axis, whole_axis, P(None, AXES, None, None), P(None, None, AXES),
            P(None, "fsdp"), weight, weight, weight, weight, weight,
        ),
        check_vma=False,
    )
```

```python
import functools

import jax
import jax.numpy as jnp
from jax import lax
from jax.experimental import pallas as pl
from jax.experimental.pallas import tpu as pltpu
from jax.sharding import PartitionSpec as P

GROUP = 16
T = 128
DOCS = 4
H = 128
P_SIZE = 64
N = 128
G = 8
HG = H // G
GC = HG * P_SIZE
GS = 2048
DI = 8192
CONV = 10240
PROMPTS = 32
AHEAD = 128
STEPS = 32752.0
Q_ROWS = 72

F32 = jnp.float32
BF16 = jnp.bfloat16
NN = (((1,), (0,)), ((), ()))
NT = (((1,), (1,)), ((), ()))
TN = (((0,), (0,)), ((), ()))
AXES = ("dp", "fsdp")


def mm(a, b, dims=NN):
    return lax.dot_general(a, b, dims, preferred_element_type=F32)


def split(a):
    hi = a.astype(BF16)
    return hi, (a - hi.astype(F32)).astype(BF16)


def mm3(a, b, dims=NN):
    ah, al = split(a)
    bh, bl = split(b)
    along, out = (1, 0) if dims == NT else (0, 1)
    n = b.shape[out]
    got = mm(cat([ah, al], 1), cat([cat([bh, bh], along), cat([bl, bl], along)], out), dims)
    return got[:, :n] + got[:, n:]


def mm3_wide(a, b):
    m, n = a.shape[0], b.shape[1]
    got = mm(cat(split(a), 0), cat(split(b), 1))
    return got[:m, :n] + (got[:m, n:] + got[m:, :n])


def cat(parts, axis):
    return jnp.concatenate(parts, axis=axis)


def sigmoid(a):
    return 1.0 / (1.0 + jnp.exp(-a))


def level(top):
    return jnp.ceil(jnp.log2(jnp.maximum(top, 1e-30)) + 0.001)


def coded(a, rung):
    return jnp.round(a * (jnp.exp2(-rung) * STEPS)).astype(jnp.int32).astype(jnp.int16)


def lanes(rows=T):
    return lax.broadcasted_iota(jnp.int32, (rows, 128), 1)


def head_sum_matrix(first):
    row = lax.broadcasted_iota(jnp.int32, (128, 128), 0)
    col = lax.broadcasted_iota(jnp.int32, (128, 128), 1)
    return (col == first + row // P_SIZE).astype(BF16)


def lagged(u, tails, sel, off):
    led = mm(sel, tails.astype(BF16))
    out = []
    for k in (1, 2, 3):
        back = jnp.where(off >= k, pltpu.roll(u, k, axis=0), 0.0)
        out.append(back + led[(k - 1) * T : k * T])
    return out


def conv_forward(raw, tails, w, bias, sel, off):
    u = raw.astype(F32)
    l1, l2, l3 = lagged(u, tails, sel, off)
    a = bias + w[3:4] * u + w[2:3] * l1 + w[1:2] * l2 + w[0:1] * l3
    sig = sigmoid(a)
    return a * sig, sig * (1.0 + a * (1.0 - sig))


def conv_backward(dout, sp, raw, tails, w, selr, off):
    u = raw.astype(F32)
    da = dout * sp
    led = mm(selr, cat(split(da), 1))
    led = led[:, :128] + led[:, 128:]
    du = w[3:4] * da
    dt = jnp.zeros((16, 128), F32)
    sums = [jnp.sum(da * u, axis=0, keepdims=True), jnp.sum(da, axis=0, keepdims=True)]
    for k in (1, 2, 3):
        tap = w[3 - k : 4 - k]
        inside = off >= k
        own = led[16 * (k - 1) : 16 * k]
        dt = dt + tap * own
        back = jnp.where(inside, pltpu.roll(u, k, axis=0), 0.0)
        part = jnp.sum(da * back, axis=0, keepdims=True)
        sums.insert(0, part + jnp.sum(own * tails, axis=0, keepdims=True))
        du = du + pltpu.roll(jnp.where(inside, tap * da, 0.0), T - k, axis=0)
    sums.append(jnp.zeros((3, 128), F32))
    return du, cat(sums, 0), dt


def color(q):
    return (q & 1) ^ (2 * ((q >> 1) & 1)) ^ (3 * ((q >> 3) & 1))


def classes(devices):
    return [[q for q in range(devices) if color(q) == k] for k in range(4)]


def local_kernel(
    xr, br, cr, tx, tb, tc, wx, wb, wc, bx, bb, bc, off_ref, sel_ref,
    caus_ref, rel_ref, relt_ref, stept_ref, dsk_ref,
    x_o, b_o, c_o, spx_o, spb_o, spc_o, m0_o, lw_o, exr_o, cq_o, sc_o, score_o,
):
    off = off_ref[...]
    sel = sel_ref[...]
    b, spb = conv_forward(br[...], tb[...], wb[...], bb[...], sel, off)
    c, spc = conv_forward(cr[...], tc[...], wc[...], bc[...], sel, off)
    b_o[...] = b
    c_o[...] = c
    spb_o[...] = spb
    spc_o[...] = spc
    scores = mm3(c, b, NT)
    score_o[0] = scores
    rung = level(jnp.max(jnp.abs(c), axis=1, keepdims=True))
    cq = coded(c, rung)
    for h in range(4):
        cq_o[h] = cq
    sc_o[0] = jnp.broadcast_to(rung, (T, T)).T[:1]
    caus = caus_ref[...] > 0.0
    first = lanes() < P_SIZE
    for i in range(HG // 2):
        at = slice(128 * i, 128 * (i + 1))
        x, spx = conv_forward(xr[:, at], tx[:, at], wx[:, at], bx[:, at], sel, off)
        x_o[:, at] = x
        spx_o[:, at] = spx
        cols, weights = [], []
        for j in (2 * i, 2 * i + 1):
            col = jnp.broadcast_to(rel_ref[0, :, j : j + 1], (T, T))
            gap = jnp.where(caus, col - relt_ref[j : j + 1, :], -1e30)
            lw = jnp.exp(gap) * stept_ref[j : j + 1, :]
            lw_o[j] = lw
            cols.append(col)
            weights.append(lw * scores)
        exr_o[:, at] = jnp.exp(jnp.where(first, cols[0], cols[1]))
        wide = cat([jnp.where(first, x, 0.0), jnp.where(first, 0.0, x)], 0)
        m0_o[:, at] = mm3_wide(cat(weights, 1), wide) + dsk_ref[:, at] * x


def norm_kernel(
    st_ref, c_ref, m0_ref, exr_ref, z_ref, up_ref, gain_ref, tokw_ref, memb_ref, sc_ref,
    dz_o, dm_o, q_o, dg_o, rs_o,
    mix_s,
):
    memb = memb_ref[...]
    tokw = tokw_ref[...]
    for gg in range(2):
        cg = c_ref[:, 128 * gg : 128 * (gg + 1)]
        hi, lo = split(cat([cg * memb[:, d : d + 1] for d in range(DOCS)], 1))
        rhs = cat(
            [st_ref[HG * gg : HG * (gg + 1), d].reshape(GC, N) for d in range(DOCS)], 1
        )
        both = mm(cat([hi, lo], 0), rhs, NT)
        at = slice(GC * gg, GC * (gg + 1))
        mix_s[:, at] = m0_ref[:, at] + (both[:T] + both[T:]) * exr_ref[:, at]
    squares = jnp.zeros((T, 128), F32)
    crossed = jnp.zeros((T, 128), F32)
    for i in range(GS // 128):
        at = slice(128 * i, 128 * (i + 1))
        z = z_ref[:, at].astype(F32)
        v = mix_s[:, at] * (z * sigmoid(z))
        dn = up_ref[:, at].astype(F32) * tokw * gain_ref[:, at]
        squares = squares + v * v
        crossed = crossed + dn * v
    r = lax.rsqrt(jnp.sum(squares, axis=1, keepdims=True) * (1.0 / GS) + 1e-05)
    k = r * r * r * (jnp.sum(crossed, axis=1, keepdims=True) * (1.0 / GS))
    r = jnp.broadcast_to(r, (T, 128))
    k = jnp.broadcast_to(k, (T, 128))
    rs = jnp.zeros((2 * T, 128), F32)
    for i in range(GS // 128):
        at = slice(128 * i, 128 * (i + 1))
        z = z_ref[:, at].astype(F32)
        sig = sigmoid(z)
        sz = z * sig
        mixed = mix_s[:, at]
        v = mixed * sz
        go = up_ref[:, at].astype(F32) * tokw
        dg_o[:, at] = jnp.broadcast_to(jnp.sum(go * v * r, axis=0, keepdims=True), (8, 128))
        dv = r * (go * gain_ref[:, at]) - v * k
        dm = dv * sz
        dm_o[:, at] = dm
        dz_o[:, at] = (dv * mixed * (sig * (1.0 + z * (1.0 - sig)))).astype(BF16)
        hi, lo = split(dm * mixed)
        rs = rs + mm(cat([hi, lo], 0), head_sum_matrix(2 * i))
        turned = (dm * exr_ref[:, at]).T
        for j in range(2):
            h = 2 * i + j
            e = turned[P_SIZE * j : P_SIZE * (j + 1)]
            rung = level(jnp.max(jnp.abs(e), axis=0, keepdims=True))
            scaled = jnp.round(e * (jnp.exp2(-rung) * STEPS))
            both = jnp.broadcast_to(rung + sc_ref[h // HG], (Q_ROWS - P_SIZE, T))
            q_o[h] = cat([scaled, both], 0).astype(jnp.int32).astype(jnp.int16)
    rs_o[...] = (rs[:T] + rs[T:]).T[:32]


def back_kernel(
    st_ref, dm_ref, exr_ref, lw_ref, score_ref, x_ref, b_ref, c_ref,
    spx, spb, spc, xr, br, cr, tx, tb, tc, wx, wb, wc, off_ref, selr_ref,
    memb_ref, dsk_ref, caus_ref, rs_ref, stept_ref, sigt_ref, rate_ref, skip_ref, dgain_ref,
    gx_o, gb_o, gc_o, gdt_o, pay_o,
    acc_s, heads_s,
):
    group = pl.program_id(0)
    off = off_ref[...]
    selr = selr_ref[...]
    memb = memb_ref[...]
    b = b_ref[...]
    c = c_ref[...]
    scores = score_ref[0]

    def keep(first, sums, dt):
        first = pl.multiple_of(AHEAD + first, 128)
        acc_s[:16, pl.ds(first, 128)] = dt
        acc_s[16:, pl.ds(first, 128)] = sums

    hi, lo = split(dm_ref[...] * exr_ref[...])
    rhs = cat([st_ref[:, d].reshape(GC, N) for d in range(DOCS)], 1)
    both = mm(cat([hi, lo], 0), rhs)
    both = both[:T] + both[T:]
    dc = jnp.zeros((T, N), F32)
    for d in range(DOCS):
        dc = dc + both[:, N * d : N * (d + 1)] * memb[:, d : d + 1]
    first = lanes() < P_SIZE
    dscores = jnp.zeros((T, T), F32)
    rx = jnp.zeros((2 * T, 128), F32)
    col_q = []
    for i in range(HG // 2):
        at = slice(128 * i, 128 * (i + 1))
        dm = dm_ref[:, at]
        x = x_ref[:, at]
        wide = cat([jnp.where(first, dm, 0.0), jnp.where(first, 0.0, dm)], 0)
        dweights = mm3(wide, x, NT)
        weights = []
        for j in range(2):
            lw = lw_ref[2 * i + j]
            g1 = dweights[T * j : T * (j + 1)] * lw
            dscores = dscores + g1
            col_q.append(jnp.sum(g1 * scores, axis=0, keepdims=True))
            weights.append(lw * scores)
        dx = mm3_wide(wide_t(dm), cat(weights, 0)).T + dsk_ref[:, at] * dm
        hi, lo = split(dm * x)
        rx = rx + mm(cat([hi, lo], 0), head_sum_matrix(2 * i))
        du, sums, dt = conv_backward(dx, spx[:, at], xr[:, at], tx[:, at], wx[:, at], selr, off)
        gx_o[:, at] = du.astype(BF16)
        keep(group * GC + 128 * i, sums, dt)

    dc = dc + mm3(dscores, b)
    db = mm3(dscores.T, c)
    du, sums, dt = conv_backward(db, spb[...], br[...], tb[...], wb[...], selr, off)
    gb_o[...] = du.astype(BF16)
    keep(DI + group * N, sums, dt)
    du, sums, dt = conv_backward(dc, spc[...], cr[...], tc[...], wc[...], selr, off)
    gc_o[...] = du.astype(BF16)
    keep(DI + G * N + group * N, sums, dt)

    rx = (rx[:T] + rx[T:]).T[:HG]
    col_q = cat(col_q, 0)
    d_rel = rs_ref[...] - skip_ref[...] * rx - col_q
    d_decay = mm(cat(three_parts(d_rel), 0), caus_ref[...].astype(BF16))
    d_decay = d_decay[:HG] + (d_decay[HG : 2 * HG] + d_decay[2 * HG :])
    step = stept_ref[...]
    rate = rate_ref[...]
    d_dt = (col_q / step - rate * d_decay) * sigt_ref[...]
    gdt_o[...] = d_dt
    lane = lanes(HG)
    heads = jnp.where(lane == 0, jnp.sum(d_dt, axis=1, keepdims=True), 0.0)
    heads = jnp.where(lane == 1, -jnp.sum(step * rate * d_decay, axis=1, keepdims=True), heads)
    heads = jnp.where(lane == 2, jnp.sum(rx, axis=1, keepdims=True), heads)
    heads_s[pl.ds(pl.multiple_of(group * HG, HG), HG), :] = heads

    @pl.when(group == G - 1)
    def _():
        acc_s[:, :AHEAD] = jnp.zeros((24, AHEAD), F32)
        acc_s[:, AHEAD + CONV :] = jnp.zeros((24, 128), F32)
        pack_gradients(acc_s, heads_s, dgain_ref, pay_o)


def window(ref, rows, at):
    base, off = at // 128 * 128, at % 128
    if off == 0:
        return ref[rows, base : base + 128]
    return pltpu.roll(ref[rows, base : base + 256], 256 - off, axis=1)[:, :128]


def pack_gradients(acc, heads, dgain, out):
    row = lax.broadcasted_iota(jnp.int32, (8, 128), 0)
    lane = lax.broadcasted_iota(jnp.int32, (8, 128), 1)
    upper = row < 4
    taps = slice(16, 24)
    for f in range(32):
        at = AHEAD + 320 * f
        w0 = pltpu.roll(window(acc, taps, at), 4, axis=0)
        w1 = window(acc, taps, at + 128)
        w2 = pltpu.roll(window(acc, taps, at + 256), 4, axis=0)
        low = dgain[:, 256 * f : 256 * f + 128]
        high = dgain[:, 256 * f + 128 : 256 * f + 256]
        g = jnp.where(row < 6, jnp.where(row < 5, pltpu.roll(low, 64, axis=1), low),
                      jnp.where(row < 7, pltpu.roll(high, 64, axis=1), high))
        last = jnp.where(upper, w1, jnp.where(lane < 64, w2, g))
        extra = jnp.zeros((8, 128), F32)
        for k in range(7):
            piece = pltpu.roll(window(acc, taps, at + 48 * k - 80), (k - 4) % 8, axis=0)
            extra = jnp.where(row == k, piece, extra)
        tile = heads[8 * (f // 2) : 8 * (f // 2) + 8, :]
        for i in range(4):
            moved = pltpu.roll(tile, 80 + 3 * i, axis=1)
            moved = pltpu.roll(moved, (7 - 4 * (f % 2) - i) % 8, axis=0)
            here = (row == 7) & (lane >= 80 + 3 * i) & (lane < 83 + 3 * i)
            extra = jnp.where(here, moved, extra)
        for p in range(4):
            m = 32 * p + f
            at = AHEAD + 80 * m
            out[m, 0:8, :] = jnp.where(lane < 80, window(acc, slice(0, 8), at), extra)
            out[m, 8:16, :] = jnp.where(upper, window(acc, slice(8, 16), at), w0)
            out[m, 16:24, :] = last


def finish_kernel(back_ref, member_ref, tails_o, w_o, b_o, g_o, heads_o):
    for j in range(3):
        rows = cat([back_ref[:, 3 * d + j, :] for d in range(DOCS)], 0)
        got = mm(member_ref[...], cat(three_parts(rows), 1))
        got = got[:, :128] + (got[:, 128:256] + got[:, 256:])
        tails_o[:, j, :] = got[:, :80]
    total = jnp.sum(back_ref[...], axis=0)
    w_o[...] = cat([total[12:16], total[16:20], total[20:24, :64]], 1)
    lane = lax.broadcasted_iota(jnp.int32, (1, 128), 1)
    turned = pltpu.roll(total[16:24], 64, axis=1)
    lo = jnp.where(lane < 64, turned[4:5], total[21:22])
    hi = jnp.where(lane < 64, turned[6:7], total[23:24])
    g_o[...] = cat([lo, hi], 1)
    row = lax.broadcasted_iota(jnp.int32, (8, 384), 0)
    wide = lax.broadcasted_iota(jnp.int32, (8, 384), 1)
    spread = cat([total[:8], jnp.zeros((8, 256), F32)], 1)
    bias = jnp.zeros((8, 384), F32)
    for k in range(7):
        here = (row == k) & (wide >= 48 * k) & (wide < 48 * k + 48)
        bias = jnp.where(here, pltpu.roll(spread, (48 * k - 80) % 384, axis=1), bias)
    b_o[...] = jnp.sum(bias, axis=0, keepdims=True)[:, :320]
    heads_o[...] = pltpu.roll(total[:8], 48, axis=1)[7:8]


def three_parts(a):
    hi, lo = split(a)
    return hi, lo, (a - hi.astype(F32) - lo.astype(F32)).astype(BF16)


def wide_t(dm):
    t = dm.T
    z = jnp.zeros((P_SIZE, T), F32)
    return cat([cat([t[:P_SIZE], z], 1), cat([z, t[P_SIZE:]], 1)], 0)


def gather_kernel(prompt_ref, table_ref, out_ref):
    step = pl.program_id(0)
    for i in range(32):
        out_ref[i] = table_ref[prompt_ref[step * 32 + i]]


def state_kernel(order_ref, prompt_ref, q_ref, c0_ref, c1_ref, c2_ref, c3_ref, mask_ref, out_ref):
    out_ref[...] = jnp.zeros_like(out_ref)

    def place(s, carry):
        for kind, c_ref in enumerate((c0_ref, c1_ref, c2_ref, c3_ref)):
            source = order_ref[kind, s]
            q = q_ref[source].astype(jnp.int32).astype(F32)
            scale = jnp.exp2(q[P_SIZE : P_SIZE + 1]) * (1.0 / STEPS**2)
            hi, lo = split(q[:P_SIZE] * scale)
            ci = c_ref[s].astype(jnp.int32)
            low = ci & 255
            high = (ci - low).astype(F32).astype(BF16)
            low = low.astype(F32).astype(BF16)
            rhs = cat([cat([high, low], 1)] * 2, 0)
            rows = []
            for d in range(DOCS):
                m = jnp.broadcast_to(mask_ref[source, d : d + 1, :], (P_SIZE, T)).astype(BF16)
                rows.append(cat([hi * m, lo * m], 1))
            got = mm(cat(rows, 0), rhs)
            got = got[:, :N] + got[:, N:]
            for d in range(DOCS):
                p = prompt_ref[source * DOCS + d]
                out_ref[p] = out_ref[p] + got[P_SIZE * d : P_SIZE * (d + 1)]
        return carry

    lax.fori_loop(0, c0_ref.shape[0], place, 0)


def whole(shape):
    return pl.BlockSpec(shape, lambda g, *_: (0,) * len(shape))


def cols(rows, width, first=0):
    return pl.BlockSpec((rows, width), lambda g, *_: (0, first + g))


def lead(*shape):
    return pl.BlockSpec(shape, lambda g, *_: (g,) + (0,) * (len(shape) - 1))


def shape(dims, dtype=F32):
    return jax.ShapeDtypeStruct(dims, dtype)


def call(body, grid, in_specs, out_specs, out_shape, name, flops, nbytes, scratch=()):
    return pl.pallas_call(
        body,
        grid=grid,
        in_specs=in_specs,
        out_specs=out_specs,
        out_shape=out_shape,
        scratch_shapes=list(scratch),
        compiler_params=pltpu.CompilerParams(vmem_limit_bytes=56 * 1024 * 1024),
        cost_estimate=pl.CostEstimate(flops=flops, bytes_accessed=nbytes, transcendentals=0),
        name=name,
    )


def three(a):
    parts = []
    for _ in range(3):
        part = lax.reduce_precision(a, 8, 7)
        parts.append(part.astype(BF16))
        a = a - part
    return parts


def advantages(rewards, resp_prompt, prompt_count):
    member = (resp_prompt[:, None] == jnp.arange(prompt_count, dtype=jnp.int32)[None, :]).astype(F32)
    group_mean = jnp.dot(rewards, member, precision=lax.Precision.HIGHEST) / GROUP
    centred = rewards - jnp.dot(member, group_mean, precision=lax.Precision.HIGHEST)
    spread = jnp.sqrt(jnp.dot(centred * centred, member, precision=lax.Precision.HIGHEST) / GROUP)
    return centred / jnp.dot(member, jnp.maximum(spread, 0.8), precision=lax.Precision.HIGHEST)


def shards(
    xbc, zgate, dt_raw, prompt_states, conv_tails, resp_prompt, resp_lengths, rewards, upstream,
    conv_weight, conv_bias, dt_bias, a_log, d_skip, norm_gain,
):
    devices = lax.axis_size("dp") * lax.axis_size("fsdp")
    n_dp, n_fsdp = lax.axis_size("dp"), lax.axis_size("fsdp")
    dp = lax.axis_index("dp")
    holder = lax.axis_index(AXES)
    exchange = functools.partial(
        lax.all_to_all, axis_name=AXES, split_axis=0, concat_axis=0, tiled=True
    )

    weights = cat(
        [conv_weight.reshape(-1), conv_bias, dt_bias, a_log, d_skip, norm_gain], 0
    )
    count = weights.shape[0]
    weights = jnp.pad(weights, (0, 2048 - count))
    quarter = lax.dynamic_slice_in_dim(weights, dp * 512, 512)
    quarter = cat(three(quarter), 0)
    onehot = resp_prompt[:, None] == jnp.arange(PROMPTS, dtype=jnp.int32)[None, :]
    tails_sent = jnp.dot(
        onehot.astype(BF16), conv_tails.reshape(PROMPTS, 240), preferred_element_type=F32
    ).astype(BF16)
    lengths_f = jnp.broadcast_to(resp_lengths.astype(BF16), (devices, DOCS))
    sent = cat(
        [
            tails_sent.reshape(devices, 960),
            lengths_f,
            jnp.zeros((devices, 60), BF16),
            jnp.broadcast_to(quarter[None], (devices, 1536)),
            jnp.zeros((devices, 512), BF16),
        ],
        1,
    )
    got = exchange(sent.reshape(devices, 24, 128)).reshape(devices, 3072)
    states = pl.pallas_call(
        gather_kernel,
        grid_spec=pltpu.PrefetchScalarGridSpec(
            num_scalar_prefetch=1,
            grid=(devices * DOCS // 32,),
            in_specs=[whole((PROMPTS, P_SIZE, N))],
            out_specs=lead(32, P_SIZE, N),
        ),
        out_shape=shape((devices * DOCS, P_SIZE, N), BF16),
        compiler_params=pltpu.CompilerParams(vmem_limit_bytes=56 * 1024 * 1024),
        cost_estimate=pl.CostEstimate(flops=0, bytes_accessed=16 * 10**6, transcendentals=0),
        name="gather_states",
    )(resp_prompt, prompt_states.reshape(PROMPTS, P_SIZE, N))
    states = exchange(states.reshape(devices, DOCS, P_SIZE, N))

    lengths, got = lax.optimization_barrier((resp_lengths[0], got))
    tails = got[:, :960].reshape(devices, 12, 80).transpose(1, 0, 2).reshape(12, CONV)
    tails = jnp.pad(tails, ((0, 4), (0, 0)))
    all_lengths = got[:, 960:964].astype(jnp.int32)
    full = sum(got[:, i : i + 512].astype(F32) for i in (2048, 1536, 1024))
    full = full.reshape(n_dp, n_fsdp, 512).transpose(1, 0, 2).reshape(n_fsdp, 2048)
    conv_w = full[:, :1280].reshape(n_fsdp, 4, 320).transpose(1, 0, 2).reshape(4, CONV)
    conv_b = full[:, 1280:1600].reshape(1, CONV)
    bias_dt = full[:, 1600:1604].reshape(1, H)
    rate = jnp.exp(full[:, 1604:1608].reshape(1, H))
    skip = full[:, 1608:1612].reshape(1, H)
    gain = full[:, 1612:1868].reshape(1, DI)

    places = jnp.arange(T, dtype=jnp.int32)
    ends = jnp.cumsum(lengths)
    starts = ends - lengths
    member = (places[:, None] >= starts[None, :]) & (places[:, None] < ends[None, :])
    start = jnp.sum(jnp.where(member, starts[None, :], 0), axis=1)
    offset = (places - start)[:, None]
    causal = ((start[:, None] == start[None, :]) & (places[:, None] >= places[None, :])).astype(F32)
    member_f = member.astype(F32)
    lag = jnp.arange(1, 4, dtype=jnp.int32)[:, None, None, None]
    row = jnp.arange(3, dtype=jnp.int32)[None, None, None, :]
    sel = member[None, :, :, None] & (offset[None, :, :, None] - lag + 3 == row)
    sel = jnp.pad(sel.reshape(3 * T, 12).astype(BF16), ((0, 0), (0, 4)))
    sel_rows = sel.reshape(3, T, 16).transpose(0, 2, 1).reshape(48, T)
    by_doc = resp_prompt.reshape(devices, DOCS).T.reshape(1, -1)
    members = (jnp.arange(PROMPTS, dtype=jnp.int32)[:, None] == by_doc).astype(BF16)
    all_ends = jnp.cumsum(all_lengths, axis=1)
    all_starts = all_ends - all_lengths
    mask_rows = (
        (places[None, None, :] >= all_starts[:, :, None])
        & (places[None, None, :] < all_ends[:, :, None])
    ).astype(F32)
    advantage = advantages(rewards, resp_prompt, PROMPTS)
    doc_weight = lax.dynamic_slice_in_dim(advantage, holder * DOCS, DOCS) * (
        T / (DOCS * lengths.astype(F32))
    )
    tokw = jnp.sum(jnp.where(member, doc_weight[None, :], 0.0), axis=1)[:, None]

    raw_step = dt_raw + bias_dt
    step = jax.nn.softplus(raw_step)
    decay = -step * rate
    rel = jnp.dot(causal, decay, precision=lax.Precision.HIGHEST)
    step_t = step.T
    rel_g = rel.reshape(T, G, HG).transpose(1, 0, 2)
    skip_wide = jnp.repeat(skip, P_SIZE, axis=1)

    groups = classes(devices)
    order = jnp.asarray(groups, jnp.int32)[color(holder) ^ jnp.arange(4, dtype=jnp.int32)]
    rate_t, skip_t, sig_t = rate.T, skip.T, jax.nn.sigmoid(raw_step).T
    (offset, sel, sel_rows, causal, member_f, members, mask_rows, tokw, order, rate_t, skip_t, sig_t, step_t,
     conv_b) = lax.optimization_barrier(
        (offset, sel, sel_rows, causal, member_f, members, mask_rows, tokw, order, rate_t, skip_t, sig_t,
         step_t, conv_b)
    )

    conv_specs = [cols(T, GC), cols(T, N, 64), cols(T, N, 72)]
    tail_specs = [cols(16, GC), cols(16, N, 64), cols(16, N, 72)]
    tap_specs = [cols(4, GC), cols(4, N, 64), cols(4, N, 72)]
    bias_specs = [cols(1, GC), cols(1, N, 64), cols(1, N, 72)]
    x, b, c, spx, spb, spc, mixed0, lw, exr, cq, sc, scores = call(
        local_kernel,
        (G,),
        conv_specs + tail_specs + tap_specs + bias_specs
        + [whole((T, 1)), whole((3 * T, 16)), whole((T, T)), lead(1, T, HG), lead(HG, T), lead(HG, T),
           cols(1, GC)],
        [cols(T, GC), cols(T, N), cols(T, N), cols(T, GC), cols(T, N), cols(T, N), cols(T, GC),
         lead(HG, T, T), cols(T, GC), lead(4, T, N), lead(1, 1, T), lead(1, T, T)],
        [shape((T, DI)), shape((T, G * N)), shape((T, G * N)), shape((T, DI)), shape((T, G * N)),
         shape((T, G * N)), shape((T, DI)), shape((H, T, T)), shape((T, DI)),
         shape((4 * G, T, N), jnp.int16), shape((G, 1, T)), shape((G, T, T))],
        "local_forward", 0, 95 * 10**6,
    )(xbc, xbc, xbc, tails, tails, tails, conv_w, conv_w, conv_w, conv_b, conv_b, conv_b,
      offset, sel, causal, rel_g, rel.T, step_t, skip_wide)

    states, cq = lax.optimization_barrier((states, cq))
    near = [lax.all_to_all(cq, AXES, 0, 0, axis_index_groups=groups, tiled=True)]
    grad_z, dm, q, d_gain, rs = call(
        norm_kernel,
        (4,),
        [lead(32, DOCS, P_SIZE, N), cols(T, 2 * N), cols(T, GS), cols(T, GS), cols(T, GS), cols(T, GS),
         cols(1, GS), whole((T, 1)), whole((T, DOCS)), lead(2, 1, T)],
        [cols(T, GS), cols(T, GS), lead(32, Q_ROWS, T), cols(8, GS), lead(32, T)],
        [shape((T, DI), BF16), shape((T, DI)), shape((H, Q_ROWS, T), jnp.int16),
         shape((8, DI)), shape((H, T))],
        "norm_both_ways", 0, 52 * 10**6,
        [pltpu.VMEM((T, GS), F32)],
    )(states, c, mixed0, exr, zgate, upstream, gain, tokw, member_f, sc)
    q, dm, near[0] = lax.optimization_barrier((q, dm, near[0]))
    for bit in (1, 2, 8):
        near.append(lax.ppermute(near[0], AXES, [(d, d ^ bit) for d in range(devices)]))
    got_q = exchange(q)

    gx, gb, gc, grad_dt, back = call(
        back_kernel,
        (G,),
        [lead(HG, DOCS, P_SIZE, N), cols(T, GC), cols(T, GC), lead(HG, T, T), lead(1, T, T),
         cols(T, GC), cols(T, N), cols(T, N), cols(T, GC), cols(T, N), cols(T, N)]
        + conv_specs + tail_specs + tap_specs
        + [whole((T, 1)), whole((48, T)), whole((T, DOCS)), cols(1, GC), whole((T, T)), lead(HG, T),
           lead(HG, T), lead(HG, T), lead(HG, 1), lead(HG, 1), whole((8, DI))],
        [cols(T, GC), cols(T, N), cols(T, N), lead(HG, T), whole((devices, 24, 128))],
        [shape((T, DI), BF16), shape((T, G * N), BF16), shape((T, G * N), BF16), shape((H, T)),
         shape((devices, 24, 128))],
        "local_backward", 0, 133 * 10**6,
        [pltpu.VMEM((24, AHEAD + CONV + 128), F32), pltpu.VMEM((H, 128), F32)],
    )(states, dm, exr, lw, scores, x, b, c, spx, spb, spc, xbc, xbc, xbc, tails, tails, tails,
      conv_w, conv_w, conv_w, offset, sel_rows, member_f, skip_wide, causal, rs, step_t,
      sig_t, rate_t, skip_t, d_gain)

    gx, gb, gc, grad_dt, back, got_q, *near = lax.optimization_barrier(
        (gx, gb, gc, grad_dt, back, got_q, *near)
    )
    grad_x = cat([gx, gb, gc], 1)
    back = exchange(back)

    grad_states = pl.pallas_call(
        state_kernel,
        grid_spec=pltpu.PrefetchScalarGridSpec(
            num_scalar_prefetch=2,
            grid=(1,),
            in_specs=[whole((devices, Q_ROWS, T))] + [whole((devices // 4, T, N))] * 4
            + [whole((devices, DOCS, T))],
            out_specs=whole((PROMPTS, P_SIZE, N)),
        ),
        out_shape=shape((PROMPTS, P_SIZE, N)),
        compiler_params=pltpu.CompilerParams(vmem_limit_bytes=56 * 1024 * 1024),
        cost_estimate=pl.CostEstimate(flops=0, bytes_accessed=60 * 10**6, transcendentals=0),
        name="state_gradients",
    )(order, resp_prompt, got_q, *near, mask_rows)

    share = CONV // n_fsdp
    grad_tails, grad_w, grad_b, grad_gain, heads = call(
        finish_kernel,
        (1,),
        [whole((devices, 24, 128)), whole((PROMPTS, devices * DOCS))],
        [whole((PROMPTS, 3, 80)), whole((4, share)), whole((1, share)), whole((1, 256)), whole((1, 128))],
        [shape((PROMPTS, 3, 80)), shape((4, share)), shape((1, share)), shape((1, 256)), shape((1, 128))],
        "finish", 0, 10 * 10**6,
    )(back, members)
    heads = heads[0, :12].reshape(4, 3)
    return (
        grad_x,
        grad_z,
        grad_dt.T,
        grad_states.reshape(PROMPTS, 1, P_SIZE, N),
        grad_tails,
        grad_w,
        grad_b.reshape(share),
        heads[:, 0],
        heads[:, 1],
        heads[:, 2],
        grad_gain.reshape(256),
    )


def solution(mesh):
    whole_axis = P(AXES, None)
    weight = P("fsdp")
    return jax.shard_map(
        shards,
        mesh=mesh,
        in_specs=(
            whole_axis, whole_axis, whole_axis, P(None, AXES, None, None), P(None, None, AXES),
            P(), whole_axis, P(), whole_axis, P(None, "fsdp"), weight, weight, weight, weight, weight,
        ),
        out_specs=(
            whole_axis, whole_axis, whole_axis, P(None, AXES, None, None), P(None, None, AXES),
            P(None, "fsdp"), weight, weight, weight, weight, weight,
        ),
        check_vma=False,
    )
```

```python
import functools

import jax
import jax.numpy as jnp
from jax import lax
from jax.experimental import pallas as pl
from jax.experimental.pallas import tpu as pltpu
from jax.sharding import PartitionSpec as P

GROUP = 16
T = 128
DOCS = 4
H = 128
P_SIZE = 64
N = 128
G = 8
HG = H // G
GC = HG * P_SIZE
GS = 2048
DI = 8192
CONV = 10240
PROMPTS = 32
AHEAD = 128
STEPS = 32752.0
Q_ROWS = 72

F32 = jnp.float32
BF16 = jnp.bfloat16
NN = (((1,), (0,)), ((), ()))
NT = (((1,), (1,)), ((), ()))
TN = (((0,), (0,)), ((), ()))
AXES = ("dp", "fsdp")


def mm(a, b, dims=NN):
    return lax.dot_general(a, b, dims, preferred_element_type=F32)


def split(a):
    hi = a.astype(BF16)
    return hi, (a - hi.astype(F32)).astype(BF16)


def mm3(a, b, dims=NN):
    ah, al = split(a)
    bh, bl = split(b)
    along, out = (1, 0) if dims == NT else (0, 1)
    n = b.shape[out]
    got = mm(cat([ah, al], 1), cat([cat([bh, bh], along), cat([bl, bl], along)], out), dims)
    return got[:, :n] + got[:, n:]


def mm3_wide(a, b):
    m, n = a.shape[0], b.shape[1]
    got = mm(cat(split(a), 0), cat(split(b), 1))
    return got[:m, :n] + (got[:m, n:] + got[m:, :n])


def cat(parts, axis):
    return jnp.concatenate(parts, axis=axis)


def sigmoid(a):
    return 1.0 / (1.0 + jnp.exp(-a))


def level(top):
    return jnp.ceil(jnp.log2(jnp.maximum(top, 1e-30)) + 0.001)


def coded(a, rung):
    return jnp.round(a * (jnp.exp2(-rung) * STEPS)).astype(jnp.int32).astype(jnp.int16)


def lanes(rows=T):
    return lax.broadcasted_iota(jnp.int32, (rows, 128), 1)


def head_sum_matrix(first):
    row = lax.broadcasted_iota(jnp.int32, (128, 128), 0)
    col = lax.broadcasted_iota(jnp.int32, (128, 128), 1)
    return (col == first + row // P_SIZE).astype(BF16)


def lagged(u, tails, sel, off):
    led = mm(sel, tails.astype(BF16))
    out = []
    for k in (1, 2, 3):
        back = jnp.where(off >= k, pltpu.roll(u, k, axis=0), 0.0)
        out.append(back + led[(k - 1) * T : k * T])
    return out


def conv_forward(raw, tails, w, bias, sel, off):
    u = raw.astype(F32)
    l1, l2, l3 = lagged(u, tails, sel, off)
    a = bias + w[3:4] * u + w[2:3] * l1 + w[1:2] * l2 + w[0:1] * l3
    sig = sigmoid(a)
    return a * sig, sig * (1.0 + a * (1.0 - sig))


def conv_backward(dout, sp, raw, tails, w, selr, off):
    u = raw.astype(F32)
    da = dout * sp
    led = mm(selr, cat(split(da), 1))
    led = led[:, :128] + led[:, 128:]
    du = w[3:4] * da
    dt = jnp.zeros((16, 128), F32)
    sums = [jnp.sum(da * u, axis=0, keepdims=True), jnp.sum(da, axis=0, keepdims=True)]
    for k in (1, 2, 3):
        tap = w[3 - k : 4 - k]
        inside = off >= k
        own = led[16 * (k - 1) : 16 * k]
        dt = dt + tap * own
        back = jnp.where(inside, pltpu.roll(u, k, axis=0), 0.0)
        part = jnp.sum(da * back, axis=0, keepdims=True)
        sums.insert(0, part + jnp.sum(own * tails, axis=0, keepdims=True))
        du = du + pltpu.roll(jnp.where(inside, tap * da, 0.0), T - k, axis=0)
    sums.append(jnp.zeros((3, 128), F32))
    return du, cat(sums, 0), dt


def color(q):
    return (q & 1) ^ (2 * ((q >> 1) & 1)) ^ (3 * ((q >> 3) & 1))


def classes(devices):
    return [[q for q in range(devices) if color(q) == k] for k in range(4)]


def local_kernel(
    xr, br, cr, tx, tb, tc, wx, wb, wc, bx, bb, bc, off_ref, sel_ref,
    caus_ref, rel_ref, relt_ref, stept_ref, dsk_ref,
    x_o, b_o, c_o, spx_o, spb_o, spc_o, m0_o, lw_o, exr_o, cq_o, sc_o, score_o,
):
    off = off_ref[...]
    sel = sel_ref[...]
    b, spb = conv_forward(br[...], tb[...], wb[...], bb[...], sel, off)
    c, spc = conv_forward(cr[...], tc[...], wc[...], bc[...], sel, off)
    b_o[...] = b
    c_o[...] = c
    spb_o[...] = spb
    spc_o[...] = spc
    scores = mm3(c, b, NT)
    score_o[0] = scores
    rung = level(jnp.max(jnp.abs(c), axis=1, keepdims=True))
    cq = coded(c, rung)
    for h in range(4):
        cq_o[h] = cq
    sc_o[0] = jnp.broadcast_to(rung, (T, T)).T[:1]
    caus = caus_ref[...] > 0.0
    first = lanes() < P_SIZE
    for i in range(HG // 2):
        at = slice(128 * i, 128 * (i + 1))
        x, spx = conv_forward(xr[:, at], tx[:, at], wx[:, at], bx[:, at], sel, off)
        x_o[:, at] = x
        spx_o[:, at] = spx
        cols, weights = [], []
        for j in (2 * i, 2 * i + 1):
            col = jnp.broadcast_to(rel_ref[0, :, j : j + 1], (T, T))
            gap = jnp.where(caus, col - relt_ref[j : j + 1, :], -1e30)
            lw = jnp.exp(gap) * stept_ref[j : j + 1, :]
            lw_o[j] = lw
            cols.append(col)
            weights.append(lw * scores)
        exr_o[:, at] = jnp.exp(jnp.where(first, cols[0], cols[1]))
        wide = cat([jnp.where(first, x, 0.0), jnp.where(first, 0.0, x)], 0)
        m0_o[:, at] = mm3_wide(cat(weights, 1), wide) + dsk_ref[:, at] * x


def norm_kernel(
    st_ref, c_ref, m0_ref, exr_ref, z_ref, up_ref, gain_ref, tokw_ref, memb_ref, sc_ref,
    dz_o, dm_o, q_o, dg_o, rs_o,
    mix_s,
):
    memb = memb_ref[...]
    tokw = tokw_ref[...]
    for gg in range(2):
        cg = c_ref[:, 128 * gg : 128 * (gg + 1)]
        hi, lo = split(cat([cg * memb[:, d : d + 1] for d in range(DOCS)], 1))
        rhs = cat(
            [st_ref[HG * gg : HG * (gg + 1), d].reshape(GC, N) for d in range(DOCS)], 1
        )
        both = mm(cat([hi, lo], 0), rhs, NT)
        at = slice(GC * gg, GC * (gg + 1))
        mix_s[:, at] = m0_ref[:, at] + (both[:T] + both[T:]) * exr_ref[:, at]
    squares = jnp.zeros((T, 128), F32)
    crossed = jnp.zeros((T, 128), F32)
    for i in range(GS // 128):
        at = slice(128 * i, 128 * (i + 1))
        z = z_ref[:, at].astype(F32)
        v = mix_s[:, at] * (z * sigmoid(z))
        dn = up_ref[:, at].astype(F32) * tokw * gain_ref[:, at]
        squares = squares + v * v
        crossed = crossed + dn * v
    r = lax.rsqrt(jnp.sum(squares, axis=1, keepdims=True) * (1.0 / GS) + 1e-05)
    k = r * r * r * (jnp.sum(crossed, axis=1, keepdims=True) * (1.0 / GS))
    r = jnp.broadcast_to(r, (T, 128))
    k = jnp.broadcast_to(k, (T, 128))
    rs = jnp.zeros((2 * T, 128), F32)
    for i in range(GS // 128):
        at = slice(128 * i, 128 * (i + 1))
        z = z_ref[:, at].astype(F32)
        sig = sigmoid(z)
        sz = z * sig
        mixed = mix_s[:, at]
        v = mixed * sz
        go = up_ref[:, at].astype(F32) * tokw
        dg_o[:, at] = jnp.broadcast_to(jnp.sum(go * v * r, axis=0, keepdims=True), (8, 128))
        dv = r * (go * gain_ref[:, at]) - v * k
        dm = dv * sz
        dm_o[:, at] = dm
        dz_o[:, at] = (dv * mixed * (sig * (1.0 + z * (1.0 - sig)))).astype(BF16)
        hi, lo = split(dm * mixed)
        rs = rs + mm(cat([hi, lo], 0), head_sum_matrix(2 * i))
        turned = (dm * exr_ref[:, at]).T
        for j in range(2):
            h = 2 * i + j
            e = turned[P_SIZE * j : P_SIZE * (j + 1)]
            rung = level(jnp.max(jnp.abs(e), axis=0, keepdims=True))
            scaled = jnp.round(e * (jnp.exp2(-rung) * STEPS))
            both = jnp.broadcast_to(rung + sc_ref[h // HG], (Q_ROWS - P_SIZE, T))
            q_o[h] = cat([scaled, both], 0).astype(jnp.int32).astype(jnp.int16)
    rs_o[...] = (rs[:T] + rs[T:]).T[:32]


def back_kernel(
    st_ref, dm_ref, exr_ref, lw_ref, score_ref, x_ref, b_ref, c_ref,
    spx, spb, spc, xr, br, cr, tx, tb, tc, wx, wb, wc, off_ref, selr_ref,
    memb_ref, dsk_ref, caus_ref, rs_ref, stept_ref, sigt_ref, rate_ref, skip_ref, dgain_ref,
    gx_o, gb_o, gc_o, gdt_o, pay_o,
    acc_s, heads_s,
):
    group = pl.program_id(0)
    off = off_ref[...]
    selr = selr_ref[...]
    memb = memb_ref[...]
    b = b_ref[...]
    c = c_ref[...]
    scores = score_ref[0]

    def keep(first, sums, dt):
        first = pl.multiple_of(AHEAD + first, 128)
        acc_s[:16, pl.ds(first, 128)] = dt
        acc_s[16:, pl.ds(first, 128)] = sums

    hi, lo = split(dm_ref[...] * exr_ref[...])
    rhs = cat([st_ref[:, d].reshape(GC, N) for d in range(DOCS)], 1)
    both = mm(cat([hi, lo], 0), rhs)
    both = both[:T] + both[T:]
    dc = jnp.zeros((T, N), F32)
    for d in range(DOCS):
        dc = dc + both[:, N * d : N * (d + 1)] * memb[:, d : d + 1]
    first = lanes() < P_SIZE
    dscores = jnp.zeros((T, T), F32)
    rx = jnp.zeros((2 * T, 128), F32)
    col_q = []
    for i in range(HG // 2):
        at = slice(128 * i, 128 * (i + 1))
        dm = dm_ref[:, at]
        x = x_ref[:, at]
        wide = cat([jnp.where(first, dm, 0.0), jnp.where(first, 0.0, dm)], 0)
        dweights = mm3(wide, x, NT)
        weights = []
        for j in range(2):
            lw = lw_ref[2 * i + j]
            g1 = dweights[T * j : T * (j + 1)] * lw
            dscores = dscores + g1
            col_q.append(jnp.sum(g1 * scores, axis=0, keepdims=True))
            weights.append(lw * scores)
        dx = mm3_wide(wide_t(dm), cat(weights, 0)).T + dsk_ref[:, at] * dm
        hi, lo = split(dm * x)
        rx = rx + mm(cat([hi, lo], 0), head_sum_matrix(2 * i))
        du, sums, dt = conv_backward(dx, spx[:, at], xr[:, at], tx[:, at], wx[:, at], selr, off)
        gx_o[:, at] = du.astype(BF16)
        keep(group * GC + 128 * i, sums, dt)

    dc = dc + mm3(dscores, b)
    db = mm3(dscores.T, c)
    du, sums, dt = conv_backward(db, spb[...], br[...], tb[...], wb[...], selr, off)
    gb_o[...] = du.astype(BF16)
    keep(DI + group * N, sums, dt)
    du, sums, dt = conv_backward(dc, spc[...], cr[...], tc[...], wc[...], selr, off)
    gc_o[...] = du.astype(BF16)
    keep(DI + G * N + group * N, sums, dt)

    rx = (rx[:T] + rx[T:]).T[:HG]
    col_q = cat(col_q, 0)
    d_rel = rs_ref[...] - skip_ref[...] * rx - col_q
    d_decay = mm(cat(three_parts(d_rel), 0), caus_ref[...].astype(BF16))
    d_decay = d_decay[:HG] + (d_decay[HG : 2 * HG] + d_decay[2 * HG :])
    step = stept_ref[...]
    rate = rate_ref[...]
    d_dt = (col_q / step - rate * d_decay) * sigt_ref[...]
    gdt_o[...] = d_dt
    lane = lanes(HG)
    heads = jnp.where(lane == 0, jnp.sum(d_dt, axis=1, keepdims=True), 0.0)
    heads = jnp.where(lane == 4, -jnp.sum(step * rate * d_decay, axis=1, keepdims=True), heads)
    heads = jnp.where(lane == 8, jnp.sum(rx, axis=1, keepdims=True), heads)
    heads_s[pl.ds(pl.multiple_of(group * HG, HG), HG), :] = heads

    @pl.when(group == G - 1)
    def _():
        acc_s[:, :AHEAD] = jnp.zeros((24, AHEAD), F32)
        acc_s[:, AHEAD + CONV :] = jnp.zeros((24, 128), F32)
        pack_gradients(acc_s, heads_s, dgain_ref, pay_o)


def window(ref, rows, at):
    base, off = at // 128 * 128, at % 128
    if off == 0:
        return ref[rows, base : base + 128]
    return pltpu.roll(ref[rows, base : base + 256], 256 - off, axis=1)[:, :128]


def pack_gradients(acc, heads, dgain, out):
    row = lax.broadcasted_iota(jnp.int32, (8, 128), 0)
    lane = lax.broadcasted_iota(jnp.int32, (8, 128), 1)
    upper = row < 4
    taps = slice(16, 24)
    for f in range(32):
        at = AHEAD + 320 * f
        w0 = pltpu.roll(window(acc, taps, at), 4, axis=0)
        w1 = window(acc, taps, at + 128)
        w2 = pltpu.roll(window(acc, taps, at + 256), 4, axis=0)
        low = dgain[:, 256 * f : 256 * f + 128]
        high = dgain[:, 256 * f + 128 : 256 * f + 256]
        g = jnp.where(row < 6, jnp.where(row < 5, pltpu.roll(low, 64, axis=1), low),
                      jnp.where(row < 7, pltpu.roll(high, 64, axis=1), high))
        last = jnp.where(upper, w1, jnp.where(lane < 64, w2, g))
        extra = jnp.zeros((8, 128), F32)
        for k in range(7):
            piece = pltpu.roll(window(acc, taps, at + 48 * k - 80), (k - 4) % 8, axis=0)
            extra = jnp.where(row == k, piece, extra)
        tile = heads[8 * (f // 2) : 8 * (f // 2) + 8, :]
        for i in range(4):
            moved = pltpu.roll(tile, 80 + i, axis=1)
            moved = pltpu.roll(moved, (7 - 4 * (f % 2) - i) % 8, axis=0)
            here = (row == 7) & (lane >= 80) & (lane < 92) & (lane % 4 == i)
            extra = jnp.where(here, moved, extra)
        for p in range(4):
            m = 32 * p + f
            at = AHEAD + 80 * m
            out[m, 0:8, :] = jnp.where(lane < 80, window(acc, slice(0, 8), at), extra)
            out[m, 8:16, :] = jnp.where(upper, window(acc, slice(8, 16), at), w0)
            out[m, 16:24, :] = last


def finish_kernel(back_ref, member_ref, tails_o, w_o, b_o, g_o, *heads_o):
    for j in range(3):
        rows = cat([back_ref[:, 3 * d + j, :] for d in range(DOCS)], 0)
        got = mm(member_ref[...], cat(three_parts(rows), 1))
        got = got[:, :128] + (got[:, 128:256] + got[:, 256:])
        tails_o[j] = got[:, :80]
    total = jnp.sum(back_ref[...], axis=0)
    w_o[...] = cat([total[12:16], total[16:20], total[20:24, :64]], 1)
    lane = lax.broadcasted_iota(jnp.int32, (1, 128), 1)
    turned = pltpu.roll(total[16:24], 64, axis=1)
    lo = jnp.where(lane < 64, turned[4:5], total[21:22])
    hi = jnp.where(lane < 64, turned[6:7], total[23:24])
    g_o[...] = cat([lo, hi], 1)
    row = lax.broadcasted_iota(jnp.int32, (8, 384), 0)
    wide = lax.broadcasted_iota(jnp.int32, (8, 384), 1)
    spread = cat([total[:8], jnp.zeros((8, 256), F32)], 1)
    bias = jnp.zeros((8, 384), F32)
    for k in range(7):
        here = (row == k) & (wide >= 48 * k) & (wide < 48 * k + 48)
        bias = jnp.where(here, pltpu.roll(spread, (48 * k - 80) % 384, axis=1), bias)
    b_o[...] = jnp.sum(bias, axis=0)[:320]
    for i in range(3):
        heads_o[i][...] = pltpu.roll(total[:8], 48 - 4 * i, axis=1)[7:8, :4]


def three_parts(a):
    hi, lo = split(a)
    return hi, lo, (a - hi.astype(F32) - lo.astype(F32)).astype(BF16)


def wide_t(dm):
    t = dm.T
    z = jnp.zeros((P_SIZE, T), F32)
    return cat([cat([t[:P_SIZE], z], 1), cat([z, t[P_SIZE:]], 1)], 0)


def gather_kernel(prompt_ref, table_ref, out_ref):
    step = pl.program_id(0)
    for i in range(32):
        out_ref[i] = table_ref[prompt_ref[step * 32 + i]]


def state_kernel(order_ref, prompt_ref, q_ref, c0_ref, c1_ref, c2_ref, c3_ref, mask_ref, out_ref):
    out_ref[...] = jnp.zeros_like(out_ref)

    def place(s, carry):
        for kind, c_ref in enumerate((c0_ref, c1_ref, c2_ref, c3_ref)):
            source = order_ref[kind, s]
            q = q_ref[source].astype(jnp.int32).astype(F32)
            scale = jnp.exp2(q[P_SIZE : P_SIZE + 1]) * (1.0 / STEPS**2)
            hi, lo = split(q[:P_SIZE] * scale)
            ci = c_ref[s].astype(jnp.int32)
            low = ci & 255
            high = (ci - low).astype(F32).astype(BF16)
            low = low.astype(F32).astype(BF16)
            rhs = cat([cat([high, low], 1)] * 2, 0)
            rows = []
            for d in range(DOCS):
                m = jnp.broadcast_to(mask_ref[source, d : d + 1, :], (P_SIZE, T)).astype(BF16)
                rows.append(cat([hi * m, lo * m], 1))
            got = mm(cat(rows, 0), rhs)
            got = got[:, :N] + got[:, N:]
            for d in range(DOCS):
                p = prompt_ref[source * DOCS + d]
                out_ref[p] = out_ref[p] + got[P_SIZE * d : P_SIZE * (d + 1)]
        return carry

    lax.fori_loop(0, c0_ref.shape[0], place, 0)


def whole(shape):
    return pl.BlockSpec(shape, lambda g, *_: (0,) * len(shape))


def cols(rows, width, first=0):
    return pl.BlockSpec((rows, width), lambda g, *_: (0, first + g))


def lead(*shape):
    return pl.BlockSpec(shape, lambda g, *_: (g,) + (0,) * (len(shape) - 1))


def shape(dims, dtype=F32):
    return jax.ShapeDtypeStruct(dims, dtype)


def call(body, grid, in_specs, out_specs, out_shape, name, flops, nbytes, scratch=()):
    return pl.pallas_call(
        body,
        grid=grid,
        in_specs=in_specs,
        out_specs=out_specs,
        out_shape=out_shape,
        scratch_shapes=list(scratch),
        compiler_params=pltpu.CompilerParams(vmem_limit_bytes=56 * 1024 * 1024),
        cost_estimate=pl.CostEstimate(flops=flops, bytes_accessed=nbytes, transcendentals=0),
        name=name,
    )


def three(a):
    parts = []
    for _ in range(3):
        part = lax.reduce_precision(a, 8, 7)
        parts.append(part.astype(BF16))
        a = a - part
    return parts


def advantages(rewards, resp_prompt, prompt_count):
    member = (resp_prompt[:, None] == jnp.arange(prompt_count, dtype=jnp.int32)[None, :]).astype(F32)
    group_mean = jnp.dot(rewards, member, precision=lax.Precision.HIGHEST) / GROUP
    centred = rewards - jnp.dot(member, group_mean, precision=lax.Precision.HIGHEST)
    spread = jnp.sqrt(jnp.dot(centred * centred, member, precision=lax.Precision.HIGHEST) / GROUP)
    return centred / jnp.dot(member, jnp.maximum(spread, 0.8), precision=lax.Precision.HIGHEST)


def shards(
    xbc, zgate, dt_raw, prompt_states, conv_tails, resp_prompt, resp_lengths, rewards, upstream,
    conv_weight, conv_bias, dt_bias, a_log, d_skip, norm_gain,
):
    devices = lax.axis_size("dp") * lax.axis_size("fsdp")
    n_dp, n_fsdp = lax.axis_size("dp"), lax.axis_size("fsdp")
    dp = lax.axis_index("dp")
    holder = lax.axis_index(AXES)
    exchange = functools.partial(
        lax.all_to_all, axis_name=AXES, split_axis=0, concat_axis=0, tiled=True
    )

    weights = cat(
        [conv_weight.reshape(-1), conv_bias, dt_bias, a_log, d_skip, norm_gain], 0
    )
    count = weights.shape[0]
    weights = jnp.pad(weights, (0, 2048 - count))
    quarter = lax.dynamic_slice_in_dim(weights, dp * 512, 512)
    parts = three(quarter)
    quarter = cat(parts[:2], 0)
    onehot = resp_prompt[:, None] == jnp.arange(PROMPTS, dtype=jnp.int32)[None, :]
    tails_sent = jnp.dot(
        onehot.astype(BF16), conv_tails.reshape(PROMPTS, 240), preferred_element_type=F32
    ).astype(BF16)
    lengths_f = jnp.broadcast_to(resp_lengths.astype(BF16), (devices, DOCS))
    sent = cat(
        [
            tails_sent.reshape(devices, 960),
            lengths_f,
            jnp.broadcast_to(jnp.pad(parts[2][64:80], (0, 44))[None], (devices, 60)),
            jnp.broadcast_to(quarter[None], (devices, 1024)),
        ],
        1,
    )
    got = exchange(sent.reshape(devices, 16, 128)).reshape(devices, 2048)
    states = pl.pallas_call(
        gather_kernel,
        grid_spec=pltpu.PrefetchScalarGridSpec(
            num_scalar_prefetch=1,
            grid=(devices * DOCS // 32,),
            in_specs=[whole((PROMPTS, P_SIZE, N))],
            out_specs=lead(32, P_SIZE, N),
        ),
        out_shape=shape((devices * DOCS, P_SIZE, N), BF16),
        compiler_params=pltpu.CompilerParams(vmem_limit_bytes=56 * 1024 * 1024),
        cost_estimate=pl.CostEstimate(flops=0, bytes_accessed=16 * 10**6, transcendentals=0),
        name="gather_states",
    )(resp_prompt, prompt_states.reshape(PROMPTS, P_SIZE, N))
    states = exchange(states.reshape(devices, DOCS, P_SIZE, N))

    lengths, got = lax.optimization_barrier((resp_lengths[0], got))
    tails = got[:, :960].reshape(devices, 12, 80).transpose(1, 0, 2).reshape(12, CONV)
    tails = jnp.pad(tails, ((0, 4), (0, 0)))
    all_lengths = got[:, 960:964].astype(jnp.int32)
    third = jnp.pad(got[:, 964:980].astype(F32), ((0, 0), (64, 432)))
    full = third + got[:, 1536:].astype(F32) + got[:, 1024:1536].astype(F32)
    full = full.reshape(n_dp, n_fsdp, 512).transpose(1, 0, 2).reshape(n_fsdp, 2048)
    conv_w = full[:, :1280].reshape(n_fsdp, 4, 320).transpose(1, 0, 2).reshape(4, CONV)
    conv_b = full[:, 1280:1600].reshape(1, CONV)
    bias_dt = full[:, 1600:1604].reshape(1, H)
    rate = jnp.exp(full[:, 1604:1608].reshape(1, H))
    skip = full[:, 1608:1612].reshape(1, H)
    gain = full[:, 1612:1868].reshape(1, DI)

    places = jnp.arange(T, dtype=jnp.int32)
    ends = jnp.cumsum(lengths)
    starts = ends - lengths
    member = (places[:, None] >= starts[None, :]) & (places[:, None] < ends[None, :])
    start = jnp.sum(jnp.where(member, starts[None, :], 0), axis=1)
    offset = (places - start)[:, None]
    causal = ((start[:, None] == start[None, :]) & (places[:, None] >= places[None, :])).astype(F32)
    member_f = member.astype(F32)
    lag = jnp.arange(1, 4, dtype=jnp.int32)[:, None, None, None]
    row = jnp.arange(3, dtype=jnp.int32)[None, None, None, :]
    sel = member[None, :, :, None] & (offset[None, :, :, None] - lag + 3 == row)
    sel = jnp.pad(sel.reshape(3 * T, 12).astype(BF16), ((0, 0), (0, 4)))
    sel_rows = sel.reshape(3, T, 16).transpose(0, 2, 1).reshape(48, T)
    by_doc = resp_prompt.reshape(devices, DOCS).T.reshape(1, -1)
    members = (jnp.arange(PROMPTS, dtype=jnp.int32)[:, None] == by_doc).astype(BF16)
    all_ends = jnp.cumsum(all_lengths, axis=1)
    all_starts = all_ends - all_lengths
    mask_rows = (
        (places[None, None, :] >= all_starts[:, :, None])
        & (places[None, None, :] < all_ends[:, :, None])
    ).astype(F32)
    advantage = advantages(rewards, resp_prompt, PROMPTS)
    doc_weight = lax.dynamic_slice_in_dim(advantage, holder * DOCS, DOCS) * (
        T / (DOCS * lengths.astype(F32))
    )
    tokw = jnp.sum(jnp.where(member, doc_weight[None, :], 0.0), axis=1)[:, None]

    raw_step = dt_raw + bias_dt
    step = jax.nn.softplus(raw_step)
    decay = -step * rate
    rel = jnp.dot(causal, decay, precision=lax.Precision.HIGHEST)
    step_t = step.T
    rel_g = rel.reshape(T, G, HG).transpose(1, 0, 2)
    skip_wide = jnp.repeat(skip, P_SIZE, axis=1)

    groups = classes(devices)
    order = jnp.asarray(groups, jnp.int32)[color(holder) ^ jnp.arange(4, dtype=jnp.int32)]
    sig_t = jax.nn.sigmoid(raw_step).T
    rate_t, skip_t = jnp.broadcast_to(rate.T, (H, 128)), jnp.broadcast_to(skip.T, (H, 128))
    tokw = jnp.broadcast_to(tokw, (T, 128))
    member_f = jnp.pad(member_f, ((0, 0), (0, 128 - DOCS)))
    (offset, sel, sel_rows, causal, member_f, members, mask_rows, tokw, order, rate_t, skip_t, sig_t, step_t,
     conv_b) = lax.optimization_barrier(
        (offset, sel, sel_rows, causal, member_f, members, mask_rows, tokw, order, rate_t, skip_t, sig_t,
         step_t, conv_b)
    )

    conv_specs = [cols(T, GC), cols(T, N, 64), cols(T, N, 72)]
    tail_specs = [cols(16, GC), cols(16, N, 64), cols(16, N, 72)]
    tap_specs = [cols(4, GC), cols(4, N, 64), cols(4, N, 72)]
    bias_specs = [cols(1, GC), cols(1, N, 64), cols(1, N, 72)]
    x, b, c, spx, spb, spc, mixed0, lw, exr, cq, sc, scores = call(
        local_kernel,
        (G,),
        conv_specs + tail_specs + tap_specs + bias_specs
        + [whole((T, 1)), whole((3 * T, 16)), whole((T, T)), lead(1, T, HG), lead(HG, T), lead(HG, T),
           cols(1, GC)],
        [cols(T, GC), cols(T, N), cols(T, N), cols(T, GC), cols(T, N), cols(T, N), cols(T, GC),
         lead(HG, T, T), cols(T, GC), lead(4, T, N), lead(1, 1, T), lead(1, T, T)],
        [shape((T, DI)), shape((T, G * N)), shape((T, G * N)), shape((T, DI)), shape((T, G * N)),
         shape((T, G * N)), shape((T, DI)), shape((H, T, T)), shape((T, DI)),
         shape((4 * G, T, N), jnp.int16), shape((G, 1, T)), shape((G, T, T))],
        "local_forward", 0, 95 * 10**6,
    )(xbc, xbc, xbc, tails, tails, tails, conv_w, conv_w, conv_w, conv_b, conv_b, conv_b,
      offset, sel, causal, rel_g, rel.T, step_t, skip_wide)

    states, cq = lax.optimization_barrier((states, cq))
    near = [lax.all_to_all(cq, AXES, 0, 0, axis_index_groups=groups, tiled=True)]
    grad_z, dm, q, d_gain, rs = call(
        norm_kernel,
        (4,),
        [lead(32, DOCS, P_SIZE, N), cols(T, 2 * N), cols(T, GS), cols(T, GS), cols(T, GS), cols(T, GS),
         cols(1, GS), whole((T, 128)), whole((T, 128)), lead(2, 1, T)],
        [cols(T, GS), cols(T, GS), lead(32, Q_ROWS, T), cols(8, GS), lead(32, T)],
        [shape((T, DI), BF16), shape((T, DI)), shape((H, Q_ROWS, T), jnp.int16),
         shape((8, DI)), shape((H, T))],
        "norm_both_ways", 0, 52 * 10**6,
        [pltpu.VMEM((T, GS), F32)],
    )(states, c, mixed0, exr, zgate, upstream, gain, tokw, member_f, sc)
    q, dm, near[0] = lax.optimization_barrier((q, dm, near[0]))
    for bit in (1, 2, 8):
        near.append(lax.ppermute(near[0], AXES, [(d, d ^ bit) for d in range(devices)]))
    got_q = exchange(q)

    gx, gb, gc, grad_dt, back = call(
        back_kernel,
        (G,),
        [lead(HG, DOCS, P_SIZE, N), cols(T, GC), cols(T, GC), lead(HG, T, T), lead(1, T, T),
         cols(T, GC), cols(T, N), cols(T, N), cols(T, GC), cols(T, N), cols(T, N)]
        + conv_specs + tail_specs + tap_specs
        + [whole((T, 1)), whole((48, T)), whole((T, 128)), cols(1, GC), whole((T, T)), lead(HG, T),
           lead(HG, T), lead(HG, T), lead(HG, 128), lead(HG, 128), whole((8, DI))],
        [cols(T, GC), cols(T, N), cols(T, N), lead(HG, T), whole((devices, 24, 128))],
        [shape((T, DI), BF16), shape((T, G * N), BF16), shape((T, G * N), BF16), shape((H, T)),
         shape((devices, 24, 128))],
        "local_backward", 0, 133 * 10**6,
        [pltpu.VMEM((24, AHEAD + CONV + 128), F32), pltpu.VMEM((H, 128), F32)],
    )(states, dm, exr, lw, scores, x, b, c, spx, spb, spc, xbc, xbc, xbc, tails, tails, tails,
      conv_w, conv_w, conv_w, offset, sel_rows, member_f, skip_wide, causal, rs, step_t,
      sig_t, rate_t, skip_t, d_gain)

    gx, gb, gc, grad_dt, back, got_q = lax.optimization_barrier((gx, gb, gc, grad_dt, back, got_q))
    grad_x = cat([gx, gb, gc], 1)
    back = exchange(back)

    grad_states = pl.pallas_call(
        state_kernel,
        grid_spec=pltpu.PrefetchScalarGridSpec(
            num_scalar_prefetch=2,
            grid=(1,),
            in_specs=[whole((devices, Q_ROWS, T))] + [whole((devices // 4, T, N))] * 4
            + [whole((devices, DOCS, T))],
            out_specs=whole((PROMPTS, P_SIZE, N)),
        ),
        out_shape=shape((PROMPTS, P_SIZE, N)),
        compiler_params=pltpu.CompilerParams(vmem_limit_bytes=56 * 1024 * 1024),
        cost_estimate=pl.CostEstimate(flops=0, bytes_accessed=60 * 10**6, transcendentals=0),
        name="state_gradients",
    )(order, resp_prompt, got_q, *near, mask_rows)

    share = CONV // n_fsdp
    grad_tails, grad_w, grad_b, grad_gain, *heads = call(
        finish_kernel,
        (1,),
        [whole((devices, 24, 128)), whole((PROMPTS, devices * DOCS))],
        [whole((3, PROMPTS, 80)), whole((4, share)), whole((share,)), whole((1, 256))] + [whole((1, 4))] * 3,
        [shape((3, PROMPTS, 80)), shape((4, share)), shape((share,)), shape((1, 256))] + [shape((1, 4))] * 3,
        "finish", 0, 10 * 10**6,
    )(back, members)
    return (
        grad_x,
        grad_z,
        grad_dt.T,
        grad_states.reshape(PROMPTS, 1, P_SIZE, N),
        grad_tails.transpose(1, 0, 2),
        grad_w,
        grad_b,
        heads[0].reshape(4),
        heads[1].reshape(4),
        heads[2].reshape(4),
        grad_gain.reshape(256),
    )


def solution(mesh):
    whole_axis = P(AXES, None)
    weight = P("fsdp")
    return jax.shard_map(
        shards,
        mesh=mesh,
        in_specs=(
            whole_axis, whole_axis, whole_axis, P(None, AXES, None, None), P(None, None, AXES),
            P(), whole_axis, P(), whole_axis, P(None, "fsdp"), weight, weight, weight, weight, weight,
        ),
        out_specs=(
            whole_axis, whole_axis, whole_axis, P(None, AXES, None, None), P(None, None, AXES),
            P(None, "fsdp"), weight, weight, weight, weight, weight,
        ),
        check_vma=False,
    )
```

```python
import functools

import jax
import jax.numpy as jnp
from jax import lax
from jax.experimental import pallas as pl
from jax.experimental.pallas import tpu as pltpu
from jax.sharding import PartitionSpec as P

GROUP = 16
T = 128
DOCS = 4
H = 128
P_SIZE = 64
N = 128
G = 8
HG = H // G
GC = HG * P_SIZE
GS = 2048
DI = 8192
CONV = 10240
PROMPTS = 32
AHEAD = 128
AT_ONCE = 8
STEPS = 32752.0
Q_ROWS = 72

F32 = jnp.float32
BF16 = jnp.bfloat16
NN = (((1,), (0,)), ((), ()))
NT = (((1,), (1,)), ((), ()))
TN = (((0,), (0,)), ((), ()))
AXES = ("dp", "fsdp")


def mm(a, b, dims=NN):
    return lax.dot_general(a, b, dims, preferred_element_type=F32)


def split(a):
    hi = a.astype(BF16)
    return hi, (a - hi.astype(F32)).astype(BF16)


def mm3(a, b, dims=NN):
    ah, al = split(a)
    bh, bl = split(b)
    along, out = (1, 0) if dims == NT else (0, 1)
    n = b.shape[out]
    got = mm(cat([ah, al], 1), cat([cat([bh, bh], along), cat([bl, bl], along)], out), dims)
    return got[:, :n] + got[:, n:]


def mm3_wide(a, b):
    m, n = a.shape[0], b.shape[1]
    got = mm(cat(split(a), 0), cat(split(b), 1))
    return got[:m, :n] + (got[:m, n:] + got[m:, :n])


def cat(parts, axis):
    return jnp.concatenate(parts, axis=axis)


def sigmoid(a):
    return 1.0 / (1.0 + jnp.exp(-a))


def level(top):
    return jnp.ceil(jnp.log2(jnp.maximum(top, 1e-30)) + 0.001)


def coded(a, rung):
    return jnp.round(a * (jnp.exp2(-rung) * STEPS)).astype(jnp.int32).astype(jnp.int16)


def lanes(rows=T):
    return lax.broadcasted_iota(jnp.int32, (rows, 128), 1)


def head_sum_matrix(first):
    row = lax.broadcasted_iota(jnp.int32, (128, 128), 0)
    col = lax.broadcasted_iota(jnp.int32, (128, 128), 1)
    return (col == first + row // P_SIZE).astype(BF16)


def lagged(u, tails, sel, off):
    led = mm(sel, tails.astype(BF16))
    out = []
    for k in (1, 2, 3):
        back = jnp.where(off >= k, pltpu.roll(u, k, axis=0), 0.0)
        out.append(back + led[(k - 1) * T : k * T])
    return out


def conv_forward(raw, tails, w, bias, sel, off):
    u = raw.astype(F32)
    l1, l2, l3 = lagged(u, tails, sel, off)
    a = bias + w[3:4] * u + w[2:3] * l1 + w[1:2] * l2 + w[0:1] * l3
    sig = sigmoid(a)
    return a * sig, sig * (1.0 + a * (1.0 - sig))


def conv_backward(dout, sp, raw, tails, w, selr, off):
    u = raw.astype(F32)
    da = dout * sp
    led = mm(selr, cat(split(da), 1))
    led = led[:, :128] + led[:, 128:]
    du = w[3:4] * da
    dt = jnp.zeros((16, 128), F32)
    sums = [jnp.sum(da * u, axis=0, keepdims=True), jnp.sum(da, axis=0, keepdims=True)]
    for k in (1, 2, 3):
        tap = w[3 - k : 4 - k]
        inside = off >= k
        own = led[16 * (k - 1) : 16 * k]
        dt = dt + tap * own
        back = jnp.where(inside, pltpu.roll(u, k, axis=0), 0.0)
        part = jnp.sum(da * back, axis=0, keepdims=True)
        sums.insert(0, part + jnp.sum(own * tails, axis=0, keepdims=True))
        du = du + pltpu.roll(jnp.where(inside, tap * da, 0.0), T - k, axis=0)
    sums.append(jnp.zeros((3, 128), F32))
    return du, cat(sums, 0), dt


def color(q):
    return (q & 1) ^ (2 * ((q >> 1) & 1)) ^ (3 * ((q >> 3) & 1))


def classes(devices):
    return [[q for q in range(devices) if color(q) == k] for k in range(4)]


def local_kernel(
    xr, br, cr, tx, tb, tc, wx, wb, wc, bx, bb, bc, off_ref, sel_ref,
    caus_ref, rel_ref, relt_ref, stept_ref, dsk_ref,
    x_o, b_o, c_o, spx_o, spb_o, spc_o, m0_o, lw_o, exr_o, cq_o, sc_o, score_o,
):
    off = off_ref[...]
    sel = sel_ref[...]
    b, spb = conv_forward(br[...], tb[...], wb[...], bb[...], sel, off)
    c, spc = conv_forward(cr[...], tc[...], wc[...], bc[...], sel, off)
    b_o[...] = b
    c_o[...] = c
    spb_o[...] = spb
    spc_o[...] = spc
    scores = mm3(c, b, NT)
    score_o[0] = scores
    rung = level(jnp.max(jnp.abs(c), axis=1, keepdims=True))
    cq = coded(c, rung)
    for h in range(4):
        cq_o[h] = cq
    sc_o[0] = jnp.broadcast_to(rung, (T, T)).T[:1]
    caus = caus_ref[...] > 0.0
    first = lanes() < P_SIZE
    for i in range(HG // 2):
        at = slice(128 * i, 128 * (i + 1))
        x, spx = conv_forward(xr[:, at], tx[:, at], wx[:, at], bx[:, at], sel, off)
        x_o[:, at] = x
        spx_o[:, at] = spx
        cols, weights = [], []
        for j in (2 * i, 2 * i + 1):
            col = jnp.broadcast_to(rel_ref[0, :, j : j + 1], (T, T))
            gap = jnp.where(caus, col - relt_ref[j : j + 1, :], -1e30)
            lw = jnp.exp(gap) * stept_ref[j : j + 1, :]
            lw_o[j] = lw
            cols.append(col)
            weights.append(lw * scores)
        exr_o[:, at] = jnp.exp(jnp.where(first, cols[0], cols[1]))
        wide = cat([jnp.where(first, x, 0.0), jnp.where(first, 0.0, x)], 0)
        m0_o[:, at] = mm3_wide(cat(weights, 1), wide) + dsk_ref[:, at] * x


def norm_kernel(
    st_ref, c_ref, m0_ref, exr_ref, z_ref, up_ref, gain_ref, tokw_ref, memb_ref, sc_ref,
    dz_o, dm_o, q_o, dg_o, rs_o,
    mix_s,
):
    memb = memb_ref[...]
    tokw = tokw_ref[...]
    for gg in range(2):
        cg = c_ref[:, 128 * gg : 128 * (gg + 1)]
        hi, lo = split(cat([cg * memb[:, d : d + 1] for d in range(DOCS)], 1))
        rhs = cat(
            [st_ref[HG * gg : HG * (gg + 1), d].reshape(GC, N) for d in range(DOCS)], 1
        )
        both = mm(cat([hi, lo], 0), rhs, NT)
        at = slice(GC * gg, GC * (gg + 1))
        mix_s[:, at] = m0_ref[:, at] + (both[:T] + both[T:]) * exr_ref[:, at]
    squares = jnp.zeros((T, 128), F32)
    crossed = jnp.zeros((T, 128), F32)
    for i in range(GS // 128):
        at = slice(128 * i, 128 * (i + 1))
        z = z_ref[:, at].astype(F32)
        v = mix_s[:, at] * (z * sigmoid(z))
        dn = up_ref[:, at].astype(F32) * tokw * gain_ref[:, at]
        squares = squares + v * v
        crossed = crossed + dn * v
    r = lax.rsqrt(jnp.sum(squares, axis=1, keepdims=True) * (1.0 / GS) + 1e-05)
    k = r * r * r * (jnp.sum(crossed, axis=1, keepdims=True) * (1.0 / GS))
    r = jnp.broadcast_to(r, (T, 128))
    k = jnp.broadcast_to(k, (T, 128))
    rs = jnp.zeros((2 * T, 128), F32)
    for i in range(GS // 128):
        at = slice(128 * i, 128 * (i + 1))
        z = z_ref[:, at].astype(F32)
        sig = sigmoid(z)
        sz = z * sig
        mixed = mix_s[:, at]
        v = mixed * sz
        go = up_ref[:, at].astype(F32) * tokw
        dg_o[:, at] = jnp.broadcast_to(jnp.sum(go * v * r, axis=0, keepdims=True), (8, 128))
        dv = r * (go * gain_ref[:, at]) - v * k
        dm = dv * sz
        dm_o[:, at] = dm
        dz_o[:, at] = (dv * mixed * (sig * (1.0 + z * (1.0 - sig)))).astype(BF16)
        hi, lo = split(dm * mixed)
        rs = rs + mm(cat([hi, lo], 0), head_sum_matrix(2 * i))
        turned = (dm * exr_ref[:, at]).T
        for j in range(2):
            h = 2 * i + j
            e = turned[P_SIZE * j : P_SIZE * (j + 1)]
            rung = level(jnp.max(jnp.abs(e), axis=0, keepdims=True))
            scaled = jnp.round(e * (jnp.exp2(-rung) * STEPS))
            both = jnp.broadcast_to(rung + sc_ref[h // HG], (Q_ROWS - P_SIZE, T))
            q_o[h] = cat([scaled, both], 0).astype(jnp.int32).astype(jnp.int16)
    rs_o[...] = (rs[:T] + rs[T:]).T[:32]


def back_kernel(
    st_ref, dm_ref, exr_ref, lw_ref, score_ref, x_ref, b_ref, c_ref,
    spx, spb, spc, xr, br, cr, tx, tb, tc, wx, wb, wc, off_ref, selr_ref,
    memb_ref, dsk_ref, caus_ref, rs_ref, stept_ref, sigt_ref, rate_ref, skip_ref, dgain_ref,
    gx_o, gb_o, gc_o, gdt_o, pay_o,
    acc_s, heads_s,
):
    group = pl.program_id(0)
    off = off_ref[...]
    selr = selr_ref[...]
    memb = memb_ref[...]
    b = b_ref[...]
    c = c_ref[...]
    scores = score_ref[0]

    def keep(first, sums, dt):
        first = pl.multiple_of(AHEAD + first, 128)
        acc_s[:16, pl.ds(first, 128)] = dt
        acc_s[16:, pl.ds(first, 128)] = sums

    hi, lo = split(dm_ref[...] * exr_ref[...])
    rhs = cat([st_ref[:, d].reshape(GC, N) for d in range(DOCS)], 1)
    both = mm(cat([hi, lo], 0), rhs)
    both = both[:T] + both[T:]
    dc = jnp.zeros((T, N), F32)
    for d in range(DOCS):
        dc = dc + both[:, N * d : N * (d + 1)] * memb[:, d : d + 1]
    first = lanes() < P_SIZE
    dscores = jnp.zeros((T, T), F32)
    rx = jnp.zeros((2 * T, 128), F32)
    col_q = []
    for i in range(HG // 2):
        at = slice(128 * i, 128 * (i + 1))
        dm = dm_ref[:, at]
        x = x_ref[:, at]
        wide = cat([jnp.where(first, dm, 0.0), jnp.where(first, 0.0, dm)], 0)
        dweights = mm3(wide, x, NT)
        weights = []
        for j in range(2):
            lw = lw_ref[2 * i + j]
            g1 = dweights[T * j : T * (j + 1)] * lw
            dscores = dscores + g1
            col_q.append(jnp.sum(g1 * scores, axis=0, keepdims=True))
            weights.append(lw * scores)
        dx = mm3_wide(wide_t(dm), cat(weights, 0)).T + dsk_ref[:, at] * dm
        hi, lo = split(dm * x)
        rx = rx + mm(cat([hi, lo], 0), head_sum_matrix(2 * i))
        du, sums, dt = conv_backward(dx, spx[:, at], xr[:, at], tx[:, at], wx[:, at], selr, off)
        gx_o[:, at] = du.astype(BF16)
        keep(group * GC + 128 * i, sums, dt)

    dc = dc + mm3(dscores, b)
    db = mm3(dscores.T, c)
    du, sums, dt = conv_backward(db, spb[...], br[...], tb[...], wb[...], selr, off)
    gb_o[...] = du.astype(BF16)
    keep(DI + group * N, sums, dt)
    du, sums, dt = conv_backward(dc, spc[...], cr[...], tc[...], wc[...], selr, off)
    gc_o[...] = du.astype(BF16)
    keep(DI + G * N + group * N, sums, dt)

    rx = (rx[:T] + rx[T:]).T[:HG]
    col_q = cat(col_q, 0)
    d_rel = rs_ref[...] - skip_ref[...] * rx - col_q
    d_decay = mm(cat(three_parts(d_rel), 0), caus_ref[...].astype(BF16))
    d_decay = d_decay[:HG] + (d_decay[HG : 2 * HG] + d_decay[2 * HG :])
    step = stept_ref[...]
    rate = rate_ref[...]
    d_dt = (col_q / step - rate * d_decay) * sigt_ref[...]
    gdt_o[...] = d_dt
    lane = lanes(HG)
    heads = jnp.where(lane == 0, jnp.sum(d_dt, axis=1, keepdims=True), 0.0)
    heads = jnp.where(lane == 4, -jnp.sum(step * rate * d_decay, axis=1, keepdims=True), heads)
    heads = jnp.where(lane == 8, jnp.sum(rx, axis=1, keepdims=True), heads)
    heads_s[pl.ds(pl.multiple_of(group * HG, HG), HG), :] = heads

    @pl.when(group == G - 1)
    def _():
        acc_s[:, :AHEAD] = jnp.zeros((24, AHEAD), F32)
        acc_s[:, AHEAD + CONV :] = jnp.zeros((24, 128), F32)
        pack_gradients(acc_s, heads_s, dgain_ref, pay_o)


def window(ref, rows, at):
    base, off = at // 128 * 128, at % 128
    if off == 0:
        return ref[rows, base : base + 128]
    return pltpu.roll(ref[rows, base : base + 256], 256 - off, axis=1)[:, :128]


def pack_gradients(acc, heads, dgain, out):
    row = lax.broadcasted_iota(jnp.int32, (8, 128), 0)
    lane = lax.broadcasted_iota(jnp.int32, (8, 128), 1)
    upper = row < 4
    taps = slice(16, 24)
    for f in range(32):
        at = AHEAD + 320 * f
        w0 = pltpu.roll(window(acc, taps, at), 4, axis=0)
        w1 = window(acc, taps, at + 128)
        w2 = pltpu.roll(window(acc, taps, at + 256), 4, axis=0)
        low = dgain[:, 256 * f : 256 * f + 128]
        high = dgain[:, 256 * f + 128 : 256 * f + 256]
        g = jnp.where(row < 6, jnp.where(row < 5, pltpu.roll(low, 64, axis=1), low),
                      jnp.where(row < 7, pltpu.roll(high, 64, axis=1), high))
        last = jnp.where(upper, w1, jnp.where(lane < 64, w2, g))
        extra = jnp.zeros((8, 128), F32)
        for k in range(7):
            piece = pltpu.roll(window(acc, taps, at + 48 * k - 80), (k - 4) % 8, axis=0)
            extra = jnp.where(row == k, piece, extra)
        tile = heads[8 * (f // 2) : 8 * (f // 2) + 8, :]
        for i in range(4):
            moved = pltpu.roll(tile, 80 + i, axis=1)
            moved = pltpu.roll(moved, (7 - 4 * (f % 2) - i) % 8, axis=0)
            here = (row == 7) & (lane >= 80) & (lane < 92) & (lane % 4 == i)
            extra = jnp.where(here, moved, extra)
        for p in range(4):
            m = 32 * p + f
            at = AHEAD + 80 * m
            out[m, 0:8, :] = jnp.where(lane < 80, window(acc, slice(0, 8), at), extra)
            out[m, 8:16, :] = jnp.where(upper, window(acc, slice(8, 16), at), w0)
            out[m, 16:24, :] = last


def finish_kernel(back_ref, member_ref, tails_o, w_o, b_o, g_o, *heads_o):
    for j in range(3):
        rows = cat([back_ref[:, 3 * d + j, :] for d in range(DOCS)], 0)
        got = mm(member_ref[...], cat(three_parts(rows), 1))
        got = got[:, :128] + (got[:, 128:256] + got[:, 256:])
        tails_o[j] = got[:, :80]
    total = jnp.sum(back_ref[...], axis=0)
    w_o[...] = cat([total[12:16], total[16:20], total[20:24, :64]], 1)
    lane = lax.broadcasted_iota(jnp.int32, (1, 128), 1)
    turned = pltpu.roll(total[16:24], 64, axis=1)
    lo = jnp.where(lane < 64, turned[4:5], total[21:22])
    hi = jnp.where(lane < 64, turned[6:7], total[23:24])
    g_o[...] = cat([lo, hi], 1)
    row = lax.broadcasted_iota(jnp.int32, (8, 384), 0)
    wide = lax.broadcasted_iota(jnp.int32, (8, 384), 1)
    spread = cat([total[:8], jnp.zeros((8, 256), F32)], 1)
    bias = jnp.zeros((8, 384), F32)
    for k in range(7):
        here = (row == k) & (wide >= 48 * k) & (wide < 48 * k + 48)
        bias = jnp.where(here, pltpu.roll(spread, (48 * k - 80) % 384, axis=1), bias)
    b_o[...] = jnp.sum(bias, axis=0)[:320]
    for i in range(3):
        heads_o[i][...] = pltpu.roll(total[:8], 48 - 4 * i, axis=1)[7:8, :4]


def three_parts(a):
    hi, lo = split(a)
    return hi, lo, (a - hi.astype(F32) - lo.astype(F32)).astype(BF16)


def wide_t(dm):
    t = dm.T
    z = jnp.zeros((P_SIZE, T), F32)
    return cat([cat([t[:P_SIZE], z], 1), cat([z, t[P_SIZE:]], 1)], 0)


def gather_kernel(prompt_ref, table_ref, out_ref):
    step = pl.program_id(0)
    for i in range(32):
        out_ref[i] = table_ref[prompt_ref[step * 32 + i]]


def state_kernel(kinds, order_ref, prompt_ref, q_ref, *refs):
    c_refs, mask_ref, rest = refs[: len(kinds)], refs[len(kinds)], refs[len(kinds) + 1 :]
    out_ref = rest[-1]
    out_ref[...] = rest[0][...] if len(rest) > 1 else jnp.zeros_like(out_ref)

    def product(source, c):
        q = q_ref[source].astype(jnp.int32).astype(F32)
        scale = jnp.exp2(q[P_SIZE : P_SIZE + 1]) * (1.0 / STEPS**2)
        hi, lo = split(q[:P_SIZE] * scale)
        ci = c.astype(jnp.int32)
        low = ci & 255
        high = (ci - low).astype(F32).astype(BF16)
        low = low.astype(F32).astype(BF16)
        rhs = cat([cat([high, low], 1)] * 2, 0)
        rows = []
        for d in range(DOCS):
            m = jnp.broadcast_to(mask_ref[source, d : d + 1, :], (P_SIZE, T)).astype(BF16)
            rows.append(cat([hi * m, lo * m], 1))
        got = mm(cat(rows, 0), rhs)
        return got[:, :N] + got[:, N:]

    def place(step, carry):
        done = []
        for i in range(AT_ONCE):
            s = step * AT_ONCE + i
            for kind, c_ref in zip(kinds, c_refs):
                source = order_ref[kind, s]
                done.append((source, product(source, c_ref[s])))
        for source, got in done:
            for d in range(DOCS):
                p = prompt_ref[source * DOCS + d]
                out_ref[p] = out_ref[p] + got[P_SIZE * d : P_SIZE * (d + 1)]
        return carry

    lax.fori_loop(0, c_refs[0].shape[0] // AT_ONCE, place, 0)


def whole(shape):
    return pl.BlockSpec(shape, lambda g, *_: (0,) * len(shape))


def cols(rows, width, first=0):
    return pl.BlockSpec((rows, width), lambda g, *_: (0, first + g))


def lead(*shape):
    return pl.BlockSpec(shape, lambda g, *_: (g,) + (0,) * (len(shape) - 1))


def shape(dims, dtype=F32):
    return jax.ShapeDtypeStruct(dims, dtype)


def call(body, grid, in_specs, out_specs, out_shape, name, flops, nbytes, scratch=()):
    return pl.pallas_call(
        body,
        grid=grid,
        in_specs=in_specs,
        out_specs=out_specs,
        out_shape=out_shape,
        scratch_shapes=list(scratch),
        compiler_params=pltpu.CompilerParams(vmem_limit_bytes=56 * 1024 * 1024),
        cost_estimate=pl.CostEstimate(flops=flops, bytes_accessed=nbytes, transcendentals=0),
        name=name,
    )


def three(a):
    parts = []
    for _ in range(3):
        part = lax.reduce_precision(a, 8, 7)
        parts.append(part.astype(BF16))
        a = a - part
    return parts


def advantages(rewards, resp_prompt, prompt_count):
    member = (resp_prompt[:, None] == jnp.arange(prompt_count, dtype=jnp.int32)[None, :]).astype(F32)
    group_mean = jnp.dot(rewards, member, precision=lax.Precision.HIGHEST) / GROUP
    centred = rewards - jnp.dot(member, group_mean, precision=lax.Precision.HIGHEST)
    spread = jnp.sqrt(jnp.dot(centred * centred, member, precision=lax.Precision.HIGHEST) / GROUP)
    return centred / jnp.dot(member, jnp.maximum(spread, 0.8), precision=lax.Precision.HIGHEST)


def shards(
    xbc, zgate, dt_raw, prompt_states, conv_tails, resp_prompt, resp_lengths, rewards, upstream,
    conv_weight, conv_bias, dt_bias, a_log, d_skip, norm_gain,
):
    devices = lax.axis_size("dp") * lax.axis_size("fsdp")
    n_dp, n_fsdp = lax.axis_size("dp"), lax.axis_size("fsdp")
    dp = lax.axis_index("dp")
    holder = lax.axis_index(AXES)
    exchange = functools.partial(
        lax.all_to_all, axis_name=AXES, split_axis=0, concat_axis=0, tiled=True
    )

    weights = cat(
        [conv_weight.reshape(-1), conv_bias, dt_bias, a_log, d_skip, norm_gain], 0
    )
    count = weights.shape[0]
    weights = jnp.pad(weights, (0, 2048 - count))
    quarter = lax.dynamic_slice_in_dim(weights, dp * 512, 512)
    parts = three(quarter)
    quarter = cat(parts[:2], 0)
    onehot = resp_prompt[:, None] == jnp.arange(PROMPTS, dtype=jnp.int32)[None, :]
    tails_sent = jnp.dot(
        onehot.astype(BF16), conv_tails.reshape(PROMPTS, 240), preferred_element_type=F32
    ).astype(BF16)
    lengths_f = jnp.broadcast_to(resp_lengths.astype(BF16), (devices, DOCS))
    sent = cat(
        [
            tails_sent.reshape(devices, 960),
            lengths_f,
            jnp.broadcast_to(jnp.pad(parts[2][64:80], (0, 44))[None], (devices, 60)),
            jnp.broadcast_to(quarter[None], (devices, 1024)),
        ],
        1,
    )
    got = exchange(sent.reshape(devices, 16, 128)).reshape(devices, 2048)
    states = pl.pallas_call(
        gather_kernel,
        grid_spec=pltpu.PrefetchScalarGridSpec(
            num_scalar_prefetch=1,
            grid=(devices * DOCS // 32,),
            in_specs=[whole((PROMPTS, P_SIZE, N))],
            out_specs=lead(32, P_SIZE, N),
        ),
        out_shape=shape((devices * DOCS, P_SIZE, N), BF16),
        compiler_params=pltpu.CompilerParams(vmem_limit_bytes=56 * 1024 * 1024),
        cost_estimate=pl.CostEstimate(flops=0, bytes_accessed=16 * 10**6, transcendentals=0),
        name="gather_states",
    )(resp_prompt, prompt_states.reshape(PROMPTS, P_SIZE, N))
    states = exchange(states.reshape(devices, DOCS, P_SIZE, N))

    lengths, got = lax.optimization_barrier((resp_lengths[0], got))
    tails = got[:, :960].reshape(devices, 12, 80).transpose(1, 0, 2).reshape(12, CONV)
    tails = jnp.pad(tails, ((0, 4), (0, 0)))
    all_lengths = got[:, 960:964].astype(jnp.int32)
    third = jnp.pad(got[:, 964:980].astype(F32), ((0, 0), (64, 432)))
    full = third + got[:, 1536:].astype(F32) + got[:, 1024:1536].astype(F32)
    full = full.reshape(n_dp, n_fsdp, 512).transpose(1, 0, 2).reshape(n_fsdp, 2048)
    conv_w = full[:, :1280].reshape(n_fsdp, 4, 320).transpose(1, 0, 2).reshape(4, CONV)
    conv_b = full[:, 1280:1600].reshape(1, CONV)
    bias_dt = full[:, 1600:1604].reshape(1, H)
    rate = jnp.exp(full[:, 1604:1608].reshape(1, H))
    skip = full[:, 1608:1612].reshape(1, H)
    gain = full[:, 1612:1868].reshape(1, DI)

    places = jnp.arange(T, dtype=jnp.int32)
    ends = jnp.cumsum(lengths)
    starts = ends - lengths
    member = (places[:, None] >= starts[None, :]) & (places[:, None] < ends[None, :])
    start = jnp.sum(jnp.where(member, starts[None, :], 0), axis=1)
    offset = (places - start)[:, None]
    causal = ((start[:, None] == start[None, :]) & (places[:, None] >= places[None, :])).astype(F32)
    member_f = member.astype(F32)
    lag = jnp.arange(1, 4, dtype=jnp.int32)[:, None, None, None]
    row = jnp.arange(3, dtype=jnp.int32)[None, None, None, :]
    sel = member[None, :, :, None] & (offset[None, :, :, None] - lag + 3 == row)
    sel = jnp.pad(sel.reshape(3 * T, 12).astype(BF16), ((0, 0), (0, 4)))
    sel_rows = sel.reshape(3, T, 16).transpose(0, 2, 1).reshape(48, T)
    by_doc = resp_prompt.reshape(devices, DOCS).T.reshape(1, -1)
    members = (jnp.arange(PROMPTS, dtype=jnp.int32)[:, None] == by_doc).astype(BF16)
    all_ends = jnp.cumsum(all_lengths, axis=1)
    all_starts = all_ends - all_lengths
    mask_rows = (
        (places[None, None, :] >= all_starts[:, :, None])
        & (places[None, None, :] < all_ends[:, :, None])
    ).astype(F32)
    advantage = advantages(rewards, resp_prompt, PROMPTS)
    doc_weight = lax.dynamic_slice_in_dim(advantage, holder * DOCS, DOCS) * (
        T / (DOCS * lengths.astype(F32))
    )
    tokw = jnp.sum(jnp.where(member, doc_weight[None, :], 0.0), axis=1)[:, None]

    raw_step = dt_raw + bias_dt
    step = jax.nn.softplus(raw_step)
    decay = -step * rate
    rel = jnp.dot(causal, decay, precision=lax.Precision.HIGHEST)
    step_t = step.T
    rel_g = rel.reshape(T, G, HG).transpose(1, 0, 2)
    skip_wide = jnp.repeat(skip, P_SIZE, axis=1)

    groups = classes(devices)
    order = jnp.asarray(groups, jnp.int32)[color(holder) ^ jnp.arange(4, dtype=jnp.int32)]
    sig_t = jax.nn.sigmoid(raw_step).T
    rate_t, skip_t = jnp.broadcast_to(rate.T, (H, 128)), jnp.broadcast_to(skip.T, (H, 128))
    tokw = jnp.broadcast_to(tokw, (T, 128))
    member_f = jnp.pad(member_f, ((0, 0), (0, 128 - DOCS)))
    (offset, sel, sel_rows, causal, member_f, members, mask_rows, tokw, order, rate_t, skip_t, sig_t, step_t,
     conv_b) = lax.optimization_barrier(
        (offset, sel, sel_rows, causal, member_f, members, mask_rows, tokw, order, rate_t, skip_t, sig_t,
         step_t, conv_b)
    )

    conv_specs = [cols(T, GC), cols(T, N, 64), cols(T, N, 72)]
    tail_specs = [cols(16, GC), cols(16, N, 64), cols(16, N, 72)]
    tap_specs = [cols(4, GC), cols(4, N, 64), cols(4, N, 72)]
    bias_specs = [cols(1, GC), cols(1, N, 64), cols(1, N, 72)]
    x, b, c, spx, spb, spc, mixed0, lw, exr, cq, sc, scores = call(
        local_kernel,
        (G,),
        conv_specs + tail_specs + tap_specs + bias_specs
        + [whole((T, 1)), whole((3 * T, 16)), whole((T, T)), lead(1, T, HG), lead(HG, T), lead(HG, T),
           cols(1, GC)],
        [cols(T, GC), cols(T, N), cols(T, N), cols(T, GC), cols(T, N), cols(T, N), cols(T, GC),
         lead(HG, T, T), cols(T, GC), lead(4, T, N), lead(1, 1, T), lead(1, T, T)],
        [shape((T, DI)), shape((T, G * N)), shape((T, G * N)), shape((T, DI)), shape((T, G * N)),
         shape((T, G * N)), shape((T, DI)), shape((H, T, T)), shape((T, DI)),
         shape((4 * G, T, N), jnp.int16), shape((G, 1, T)), shape((G, T, T))],
        "local_forward", 0, 95 * 10**6,
    )(xbc, xbc, xbc, tails, tails, tails, conv_w, conv_w, conv_w, conv_b, conv_b, conv_b,
      offset, sel, causal, rel_g, rel.T, step_t, skip_wide)

    states, cq = lax.optimization_barrier((states, cq))
    near = [lax.all_to_all(cq, AXES, 0, 0, axis_index_groups=groups, tiled=True)]
    grad_z, dm, q, d_gain, rs = call(
        norm_kernel,
        (4,),
        [lead(32, DOCS, P_SIZE, N), cols(T, 2 * N), cols(T, GS), cols(T, GS), cols(T, GS), cols(T, GS),
         cols(1, GS), whole((T, 128)), whole((T, 128)), lead(2, 1, T)],
        [cols(T, GS), cols(T, GS), lead(32, Q_ROWS, T), cols(8, GS), lead(32, T)],
        [shape((T, DI), BF16), shape((T, DI)), shape((H, Q_ROWS, T), jnp.int16),
         shape((8, DI)), shape((H, T))],
        "norm_both_ways", 0, 52 * 10**6,
        [pltpu.VMEM((T, GS), F32)],
    )(states, c, mixed0, exr, zgate, upstream, gain, tokw, member_f, sc)
    q, dm, near[0] = lax.optimization_barrier((q, dm, near[0]))
    for bit in (1, 2, 8):
        near.append(lax.ppermute(near[0], AXES, [(d, d ^ bit) for d in range(devices)]))
    got_q = exchange(q)

    gx, gb, gc, grad_dt, back = call(
        back_kernel,
        (G,),
        [lead(HG, DOCS, P_SIZE, N), cols(T, GC), cols(T, GC), lead(HG, T, T), lead(1, T, T),
         cols(T, GC), cols(T, N), cols(T, N), cols(T, GC), cols(T, N), cols(T, N)]
        + conv_specs + tail_specs + tap_specs
        + [whole((T, 1)), whole((48, T)), whole((T, 128)), cols(1, GC), whole((T, T)), lead(HG, T),
           lead(HG, T), lead(HG, T), lead(HG, 128), lead(HG, 128), whole((8, DI))],
        [cols(T, GC), cols(T, N), cols(T, N), lead(HG, T), whole((devices, 24, 128))],
        [shape((T, DI), BF16), shape((T, G * N), BF16), shape((T, G * N), BF16), shape((H, T)),
         shape((devices, 24, 128))],
        "local_backward", 0, 133 * 10**6,
        [pltpu.VMEM((24, AHEAD + CONV + 128), F32), pltpu.VMEM((H, 128), F32)],
    )(states, dm, exr, lw, scores, x, b, c, spx, spb, spc, xbc, xbc, xbc, tails, tails, tails,
      conv_w, conv_w, conv_w, offset, sel_rows, member_f, skip_wide, causal, rs, step_t,
      sig_t, rate_t, skip_t, d_gain)

    gx, gb, gc, grad_dt, back, got_q = lax.optimization_barrier((gx, gb, gc, grad_dt, back, got_q))
    grad_x = cat([gx, gb, gc], 1)
    back = exchange(back)

    def add_states(kinds, *before):
        return pl.pallas_call(
            functools.partial(state_kernel, kinds),
            grid_spec=pltpu.PrefetchScalarGridSpec(
                num_scalar_prefetch=2,
                grid=(1,),
                in_specs=[whole((devices, Q_ROWS, T))] + [whole((devices // 4, T, N))] * len(kinds)
                + [whole((devices, DOCS, T))] + [whole((PROMPTS, P_SIZE, N))] * len(before),
                out_specs=whole((PROMPTS, P_SIZE, N)),
            ),
            out_shape=shape((PROMPTS, P_SIZE, N)),
            compiler_params=pltpu.CompilerParams(vmem_limit_bytes=56 * 1024 * 1024),
            cost_estimate=pl.CostEstimate(
                flops=0, bytes_accessed=15 * 10**6 * len(kinds), transcendentals=0
            ),
            name="state_gradients_%d" % len(kinds),
        )(order, resp_prompt, got_q, *[near[k] for k in kinds], mask_rows, *before)

    grad_states = add_states((0,))
    grad_states = add_states((1, 2, 3), grad_states)

    share = CONV // n_fsdp
    grad_tails, grad_w, grad_b, grad_gain, *heads = call(
        finish_kernel,
        (1,),
        [whole((devices, 24, 128)), whole((PROMPTS, devices * DOCS))],
        [whole((3, PROMPTS, 80)), whole((4, share)), whole((share,)), whole((1, 256))] + [whole((1, 4))] * 3,
        [shape((3, PROMPTS, 80)), shape((4, share)), shape((share,)), shape((1, 256))] + [shape((1, 4))] * 3,
        "finish", 0, 10 * 10**6,
    )(back, members)
    return (
        grad_x,
        grad_z,
        grad_dt.T,
        grad_states.reshape(PROMPTS, 1, P_SIZE, N),
        grad_tails.transpose(1, 0, 2),
        grad_w,
        grad_b,
        heads[0].reshape(4),
        heads[1].reshape(4),
        heads[2].reshape(4),
        grad_gain.reshape(256),
    )


def solution(mesh):
    whole_axis = P(AXES, None)
    weight = P("fsdp")
    return jax.shard_map(
        shards,
        mesh=mesh,
        in_specs=(
            whole_axis, whole_axis, whole_axis, P(None, AXES, None, None), P(None, None, AXES),
            P(), whole_axis, P(), whole_axis, P(None, "fsdp"), weight, weight, weight, weight, weight,
        ),
        out_specs=(
            whole_axis, whole_axis, whole_axis, P(None, AXES, None, None), P(None, None, AXES),
            P(None, "fsdp"), weight, weight, weight, weight, weight,
        ),
        check_vma=False,
    )
```

```python
import functools

import jax
import jax.numpy as jnp
from jax import lax
from jax.experimental import pallas as pl
from jax.experimental.pallas import tpu as pltpu
from jax.sharding import PartitionSpec as P

GROUP = 16
T = 128
DOCS = 4
H = 128
P_SIZE = 64
N = 128
G = 8
HG = H // G
GC = HG * P_SIZE
GS = 2048
DI = 8192
CONV = 10240
PROMPTS = 32
AHEAD = 128
AT_ONCE = 16
STEPS = 32752.0
Q_ROWS = 72

F32 = jnp.float32
BF16 = jnp.bfloat16
NN = (((1,), (0,)), ((), ()))
NT = (((1,), (1,)), ((), ()))
TN = (((0,), (0,)), ((), ()))
AXES = ("dp", "fsdp")


def mm(a, b, dims=NN):
    return lax.dot_general(a, b, dims, preferred_element_type=F32)


def split(a):
    hi = a.astype(BF16)
    return hi, (a - hi.astype(F32)).astype(BF16)


def mm3(a, b, dims=NN):
    ah, al = split(a)
    bh, bl = split(b)
    along, out = (1, 0) if dims == NT else (0, 1)
    n = b.shape[out]
    got = mm(cat([ah, al], 1), cat([cat([bh, bh], along), cat([bl, bl], along)], out), dims)
    return got[:, :n] + got[:, n:]


def mm3_wide(a, b):
    m, n = a.shape[0], b.shape[1]
    got = mm(cat(split(a), 0), cat(split(b), 1))
    return got[:m, :n] + (got[:m, n:] + got[m:, :n])


def cat(parts, axis):
    return jnp.concatenate(parts, axis=axis)


def sigmoid(a):
    return 1.0 / (1.0 + jnp.exp(-a))


def level(top):
    return jnp.ceil(jnp.log2(jnp.maximum(top, 1e-30)) + 0.001)


def coded(a, rung):
    return jnp.round(a * (jnp.exp2(-rung) * STEPS)).astype(jnp.int32).astype(jnp.int16)


def lanes(rows=T):
    return lax.broadcasted_iota(jnp.int32, (rows, 128), 1)


def head_sum_matrix(first):
    row = lax.broadcasted_iota(jnp.int32, (128, 128), 0)
    col = lax.broadcasted_iota(jnp.int32, (128, 128), 1)
    return (col == first + row // P_SIZE).astype(BF16)


def lagged(u, tails, sel, off):
    led = mm(sel, tails.astype(BF16))
    out = []
    for k in (1, 2, 3):
        back = jnp.where(off >= k, pltpu.roll(u, k, axis=0), 0.0)
        out.append(back + led[(k - 1) * T : k * T])
    return out


def conv_forward(raw, tails, w, bias, sel, off):
    u = raw.astype(F32)
    l1, l2, l3 = lagged(u, tails, sel, off)
    a = bias + w[3:4] * u + w[2:3] * l1 + w[1:2] * l2 + w[0:1] * l3
    sig = sigmoid(a)
    return a * sig, sig * (1.0 + a * (1.0 - sig))


def conv_backward(dout, sp, raw, tails, w, selr, off):
    u = raw.astype(F32)
    da = dout * sp
    led = mm(selr, cat(split(da), 1))
    led = led[:, :128] + led[:, 128:]
    du = w[3:4] * da
    dt = jnp.zeros((16, 128), F32)
    sums = [jnp.sum(da * u, axis=0, keepdims=True), jnp.sum(da, axis=0, keepdims=True)]
    for k in (1, 2, 3):
        tap = w[3 - k : 4 - k]
        inside = off >= k
        own = led[16 * (k - 1) : 16 * k]
        dt = dt + tap * own
        back = jnp.where(inside, pltpu.roll(u, k, axis=0), 0.0)
        part = jnp.sum(da * back, axis=0, keepdims=True)
        sums.insert(0, part + jnp.sum(own * tails, axis=0, keepdims=True))
        du = du + pltpu.roll(jnp.where(inside, tap * da, 0.0), T - k, axis=0)
    sums.append(jnp.zeros((3, 128), F32))
    return du, cat(sums, 0), dt


def color(q):
    return (q & 1) ^ (2 * ((q >> 1) & 1)) ^ (3 * ((q >> 3) & 1))


def classes(devices):
    return [[q for q in range(devices) if color(q) == k] for k in range(4)]


def local_kernel(
    xr, br, cr, tx, tb, tc, wx, wb, wc, bx, bb, bc, off_ref, sel_ref,
    caus_ref, rel_ref, relt_ref, stept_ref, dsk_ref,
    x_o, b_o, c_o, spx_o, spb_o, spc_o, m0_o, lw_o, exr_o, cq_o, sc_o, score_o,
):
    off = off_ref[...]
    sel = sel_ref[...]
    b, spb = conv_forward(br[...], tb[...], wb[...], bb[...], sel, off)
    c, spc = conv_forward(cr[...], tc[...], wc[...], bc[...], sel, off)
    b_o[...] = b
    c_o[...] = c
    spb_o[...] = spb
    spc_o[...] = spc
    scores = mm3(c, b, NT)
    score_o[0] = scores
    rung = level(jnp.max(jnp.abs(c), axis=1, keepdims=True))
    cq = coded(c, rung)
    for h in range(4):
        cq_o[h] = cq
    sc_o[0] = jnp.broadcast_to(rung, (T, T)).T[:1]
    caus = caus_ref[...] > 0.0
    first = lanes() < P_SIZE
    for i in range(HG // 2):
        at = slice(128 * i, 128 * (i + 1))
        x, spx = conv_forward(xr[:, at], tx[:, at], wx[:, at], bx[:, at], sel, off)
        x_o[:, at] = x
        spx_o[:, at] = spx
        cols, weights = [], []
        for j in (2 * i, 2 * i + 1):
            col = jnp.broadcast_to(rel_ref[0, :, j : j + 1], (T, T))
            gap = jnp.where(caus, col - relt_ref[j : j + 1, :], -1e30)
            lw = jnp.exp(gap) * stept_ref[j : j + 1, :]
            lw_o[j] = lw
            cols.append(col)
            weights.append(lw * scores)
        exr_o[:, at] = jnp.exp(jnp.where(first, cols[0], cols[1]))
        wide = cat([jnp.where(first, x, 0.0), jnp.where(first, 0.0, x)], 0)
        m0_o[:, at] = mm3_wide(cat(weights, 1), wide) + dsk_ref[:, at] * x


def norm_kernel(
    st_ref, c_ref, m0_ref, exr_ref, z_ref, up_ref, gain_ref, tokw_ref, memb_ref, sc_ref,
    dz_o, dm_o, q_o, dg_o, rs_o,
    mix_s,
):
    memb = memb_ref[...]
    tokw = tokw_ref[...]
    for gg in range(2):
        cg = c_ref[:, 128 * gg : 128 * (gg + 1)]
        hi, lo = split(cat([cg * memb[:, d : d + 1] for d in range(DOCS)], 1))
        rhs = cat(
            [st_ref[HG * gg : HG * (gg + 1), d].reshape(GC, N) for d in range(DOCS)], 1
        )
        both = mm(cat([hi, lo], 0), rhs, NT)
        at = slice(GC * gg, GC * (gg + 1))
        mix_s[:, at] = m0_ref[:, at] + (both[:T] + both[T:]) * exr_ref[:, at]
    squares = jnp.zeros((T, 128), F32)
    crossed = jnp.zeros((T, 128), F32)
    for i in range(GS // 128):
        at = slice(128 * i, 128 * (i + 1))
        z = z_ref[:, at].astype(F32)
        v = mix_s[:, at] * (z * sigmoid(z))
        dn = up_ref[:, at].astype(F32) * tokw * gain_ref[:, at]
        squares = squares + v * v
        crossed = crossed + dn * v
    r = lax.rsqrt(jnp.sum(squares, axis=1, keepdims=True) * (1.0 / GS) + 1e-05)
    k = r * r * r * (jnp.sum(crossed, axis=1, keepdims=True) * (1.0 / GS))
    r = jnp.broadcast_to(r, (T, 128))
    k = jnp.broadcast_to(k, (T, 128))
    rs = jnp.zeros((2 * T, 128), F32)
    for i in range(GS // 128):
        at = slice(128 * i, 128 * (i + 1))
        z = z_ref[:, at].astype(F32)
        sig = sigmoid(z)
        sz = z * sig
        mixed = mix_s[:, at]
        v = mixed * sz
        go = up_ref[:, at].astype(F32) * tokw
        dg_o[:, at] = jnp.broadcast_to(jnp.sum(go * v * r, axis=0, keepdims=True), (8, 128))
        dv = r * (go * gain_ref[:, at]) - v * k
        dm = dv * sz
        dm_o[:, at] = dm
        dz_o[:, at] = (dv * mixed * (sig * (1.0 + z * (1.0 - sig)))).astype(BF16)
        hi, lo = split(dm * mixed)
        rs = rs + mm(cat([hi, lo], 0), head_sum_matrix(2 * i))
        turned = (dm * exr_ref[:, at]).T
        for j in range(2):
            h = 2 * i + j
            e = turned[P_SIZE * j : P_SIZE * (j + 1)]
            rung = level(jnp.max(jnp.abs(e), axis=0, keepdims=True))
            scaled = jnp.round(e * (jnp.exp2(-rung) * STEPS))
            both = jnp.broadcast_to(rung + sc_ref[h // HG], (Q_ROWS - P_SIZE, T))
            q_o[h] = cat([scaled, both], 0).astype(jnp.int32).astype(jnp.int16)
    rs_o[...] = (rs[:T] + rs[T:]).T[:32]


def back_kernel(
    st_ref, dm_ref, exr_ref, lw_ref, score_ref, x_ref, b_ref, c_ref,
    spx, spb, spc, xr, br, cr, tx, tb, tc, wx, wb, wc, off_ref, selr_ref,
    memb_ref, dsk_ref, caus_ref, rs_ref, stept_ref, sigt_ref, rate_ref, skip_ref, dgain_ref,
    gx_o, gb_o, gc_o, gdt_o, pay_o,
    acc_s, heads_s,
):
    group = pl.program_id(0)
    off = off_ref[...]
    selr = selr_ref[...]
    memb = memb_ref[...]
    b = b_ref[...]
    c = c_ref[...]
    scores = score_ref[0]

    def keep(first, sums, dt):
        first = pl.multiple_of(AHEAD + first, 128)
        acc_s[:16, pl.ds(first, 128)] = dt
        acc_s[16:, pl.ds(first, 128)] = sums

    hi, lo = split(dm_ref[...] * exr_ref[...])
    rhs = cat([st_ref[:, d].reshape(GC, N) for d in range(DOCS)], 1)
    both = mm(cat([hi, lo], 0), rhs)
    both = both[:T] + both[T:]
    dc = jnp.zeros((T, N), F32)
    for d in range(DOCS):
        dc = dc + both[:, N * d : N * (d + 1)] * memb[:, d : d + 1]
    first = lanes() < P_SIZE
    dscores = jnp.zeros((T, T), F32)
    rx = jnp.zeros((2 * T, 128), F32)
    col_q = []
    for i in range(HG // 2):
        at = slice(128 * i, 128 * (i + 1))
        dm = dm_ref[:, at]
        x = x_ref[:, at]
        wide = cat([jnp.where(first, dm, 0.0), jnp.where(first, 0.0, dm)], 0)
        dweights = mm3(wide, x, NT)
        weights = []
        for j in range(2):
            lw = lw_ref[2 * i + j]
            g1 = dweights[T * j : T * (j + 1)] * lw
            dscores = dscores + g1
            col_q.append(jnp.sum(g1 * scores, axis=0, keepdims=True))
            weights.append(lw * scores)
        dx = mm3_wide(wide_t(dm), cat(weights, 0)).T + dsk_ref[:, at] * dm
        hi, lo = split(dm * x)
        rx = rx + mm(cat([hi, lo], 0), head_sum_matrix(2 * i))
        du, sums, dt = conv_backward(dx, spx[:, at], xr[:, at], tx[:, at], wx[:, at], selr, off)
        gx_o[:, at] = du.astype(BF16)
        keep(group * GC + 128 * i, sums, dt)

    dc = dc + mm3(dscores, b)
    db = mm3(dscores.T, c)
    du, sums, dt = conv_backward(db, spb[...], br[...], tb[...], wb[...], selr, off)
    gb_o[...] = du.astype(BF16)
    keep(DI + group * N, sums, dt)
    du, sums, dt = conv_backward(dc, spc[...], cr[...], tc[...], wc[...], selr, off)
    gc_o[...] = du.astype(BF16)
    keep(DI + G * N + group * N, sums, dt)

    rx = (rx[:T] + rx[T:]).T[:HG]
    col_q = cat(col_q, 0)
    d_rel = rs_ref[...] - skip_ref[...] * rx - col_q
    d_decay = mm(cat(three_parts(d_rel), 0), caus_ref[...].astype(BF16))
    d_decay = d_decay[:HG] + (d_decay[HG : 2 * HG] + d_decay[2 * HG :])
    step = stept_ref[...]
    rate = rate_ref[...]
    d_dt = (col_q / step - rate * d_decay) * sigt_ref[...]
    gdt_o[...] = d_dt
    lane = lanes(HG)
    heads = jnp.where(lane == 0, jnp.sum(d_dt, axis=1, keepdims=True), 0.0)
    heads = jnp.where(lane == 4, -jnp.sum(step * rate * d_decay, axis=1, keepdims=True), heads)
    heads = jnp.where(lane == 8, jnp.sum(rx, axis=1, keepdims=True), heads)
    heads_s[pl.ds(pl.multiple_of(group * HG, HG), HG), :] = heads

    @pl.when(group == G - 1)
    def _():
        acc_s[:, :AHEAD] = jnp.zeros((24, AHEAD), F32)
        acc_s[:, AHEAD + CONV :] = jnp.zeros((24, 128), F32)
        pack_gradients(acc_s, heads_s, dgain_ref, pay_o)


def window(ref, rows, at):
    base, off = at // 128 * 128, at % 128
    if off == 0:
        return ref[rows, base : base + 128]
    return pltpu.roll(ref[rows, base : base + 256], 256 - off, axis=1)[:, :128]


def pack_gradients(acc, heads, dgain, out):
    row = lax.broadcasted_iota(jnp.int32, (8, 128), 0)
    lane = lax.broadcasted_iota(jnp.int32, (8, 128), 1)
    upper = row < 4
    taps = slice(16, 24)
    for f in range(32):
        at = AHEAD + 320 * f
        w0 = pltpu.roll(window(acc, taps, at), 4, axis=0)
        w1 = window(acc, taps, at + 128)
        w2 = pltpu.roll(window(acc, taps, at + 256), 4, axis=0)
        low = dgain[:, 256 * f : 256 * f + 128]
        high = dgain[:, 256 * f + 128 : 256 * f + 256]
        g = jnp.where(row < 6, jnp.where(row < 5, pltpu.roll(low, 64, axis=1), low),
                      jnp.where(row < 7, pltpu.roll(high, 64, axis=1), high))
        last = jnp.where(upper, w1, jnp.where(lane < 64, w2, g))
        extra = jnp.zeros((8, 128), F32)
        for k in range(7):
            piece = pltpu.roll(window(acc, taps, at + 48 * k - 80), (k - 4) % 8, axis=0)
            extra = jnp.where(row == k, piece, extra)
        tile = heads[8 * (f // 2) : 8 * (f // 2) + 8, :]
        for i in range(4):
            moved = pltpu.roll(tile, 80 + i, axis=1)
            moved = pltpu.roll(moved, (7 - 4 * (f % 2) - i) % 8, axis=0)
            here = (row == 7) & (lane >= 80) & (lane < 92) & (lane % 4 == i)
            extra = jnp.where(here, moved, extra)
        for p in range(4):
            m = 32 * p + f
            at = AHEAD + 80 * m
            out[m, 0:8, :] = jnp.where(lane < 80, window(acc, slice(0, 8), at), extra)
            out[m, 8:16, :] = jnp.where(upper, window(acc, slice(8, 16), at), w0)
            out[m, 16:24, :] = last


def finish_kernel(back_ref, member_ref, tails_o, w_o, b_o, g_o, *heads_o):
    for j in range(3):
        rows = cat([back_ref[:, 3 * d + j, :] for d in range(DOCS)], 0)
        got = mm(member_ref[...], cat(three_parts(rows), 1))
        got = got[:, :128] + (got[:, 128:256] + got[:, 256:])
        tails_o[j] = got[:, :80]
    total = jnp.sum(back_ref[...], axis=0)
    w_o[...] = cat([total[12:16], total[16:20], total[20:24, :64]], 1)
    lane = lax.broadcasted_iota(jnp.int32, (1, 128), 1)
    turned = pltpu.roll(total[16:24], 64, axis=1)
    lo = jnp.where(lane < 64, turned[4:5], total[21:22])
    hi = jnp.where(lane < 64, turned[6:7], total[23:24])
    g_o[...] = cat([lo, hi], 1)
    row = lax.broadcasted_iota(jnp.int32, (8, 384), 0)
    wide = lax.broadcasted_iota(jnp.int32, (8, 384), 1)
    spread = cat([total[:8], jnp.zeros((8, 256), F32)], 1)
    bias = jnp.zeros((8, 384), F32)
    for k in range(7):
        here = (row == k) & (wide >= 48 * k) & (wide < 48 * k + 48)
        bias = jnp.where(here, pltpu.roll(spread, (48 * k - 80) % 384, axis=1), bias)
    b_o[...] = jnp.sum(bias, axis=0)[:320]
    for i in range(3):
        heads_o[i][...] = pltpu.roll(total[:8], 48 - 4 * i, axis=1)[7:8, :4]


def three_parts(a):
    hi, lo = split(a)
    return hi, lo, (a - hi.astype(F32) - lo.astype(F32)).astype(BF16)


def wide_t(dm):
    t = dm.T
    z = jnp.zeros((P_SIZE, T), F32)
    return cat([cat([t[:P_SIZE], z], 1), cat([z, t[P_SIZE:]], 1)], 0)


def gather_kernel(prompt_ref, table_ref, out_ref):
    step = pl.program_id(0)
    for i in range(32):
        out_ref[i] = table_ref[prompt_ref[step * 32 + i]]


def state_kernel(kinds, order_ref, prompt_ref, q_ref, *refs):
    c_refs, mask_ref, rest = refs[: len(kinds)], refs[len(kinds)], refs[len(kinds) + 1 :]
    out_ref = rest[-1]
    out_ref[...] = rest[0][...] if len(rest) > 1 else jnp.zeros_like(out_ref)

    def product(source, c):
        q = q_ref[source].astype(jnp.int32).astype(F32)
        scale = jnp.exp2(q[P_SIZE : P_SIZE + 1]) * (1.0 / STEPS**2)
        hi, lo = split(q[:P_SIZE] * scale)
        ci = c.astype(jnp.int32)
        low = ci & 255
        high = (ci - low).astype(F32).astype(BF16)
        low = low.astype(F32).astype(BF16)
        rhs = cat([cat([high, low], 1)] * 2, 0)
        rows = []
        for d in range(DOCS):
            m = jnp.broadcast_to(mask_ref[source, d : d + 1, :], (P_SIZE, T)).astype(BF16)
            rows.append(cat([hi * m, lo * m], 1))
        got = mm(cat(rows, 0), rhs)
        return got[:, :N] + got[:, N:]

    def place(step, carry):
        done = []
        for i in range(AT_ONCE):
            s = step * AT_ONCE + i
            for kind, c_ref in zip(kinds, c_refs):
                source = order_ref[kind, s]
                done.append((source, product(source, c_ref[s])))
        for source, got in done:
            for d in range(DOCS):
                p = prompt_ref[source * DOCS + d]
                out_ref[p] = out_ref[p] + got[P_SIZE * d : P_SIZE * (d + 1)]
        return carry

    lax.fori_loop(0, c_refs[0].shape[0] // AT_ONCE, place, 0)


def whole(shape):
    return pl.BlockSpec(shape, lambda g, *_: (0,) * len(shape))


def cols(rows, width, first=0):
    return pl.BlockSpec((rows, width), lambda g, *_: (0, first + g))


def lead(*shape):
    return pl.BlockSpec(shape, lambda g, *_: (g,) + (0,) * (len(shape) - 1))


def shape(dims, dtype=F32):
    return jax.ShapeDtypeStruct(dims, dtype)


def call(body, grid, in_specs, out_specs, out_shape, name, flops, nbytes, scratch=()):
    return pl.pallas_call(
        body,
        grid=grid,
        in_specs=in_specs,
        out_specs=out_specs,
        out_shape=out_shape,
        scratch_shapes=list(scratch),
        compiler_params=pltpu.CompilerParams(vmem_limit_bytes=56 * 1024 * 1024),
        cost_estimate=pl.CostEstimate(flops=flops, bytes_accessed=nbytes, transcendentals=0),
        name=name,
    )


def three(a):
    parts = []
    for _ in range(3):
        part = lax.reduce_precision(a, 8, 7)
        parts.append(part.astype(BF16))
        a = a - part
    return parts


def advantages(rewards, resp_prompt, prompt_count):
    member = (resp_prompt[:, None] == jnp.arange(prompt_count, dtype=jnp.int32)[None, :]).astype(F32)
    group_mean = jnp.dot(rewards, member, precision=lax.Precision.HIGHEST) / GROUP
    centred = rewards - jnp.dot(member, group_mean, precision=lax.Precision.HIGHEST)
    spread = jnp.sqrt(jnp.dot(centred * centred, member, precision=lax.Precision.HIGHEST) / GROUP)
    return centred / jnp.dot(member, jnp.maximum(spread, 0.8), precision=lax.Precision.HIGHEST)


def shards(
    xbc, zgate, dt_raw, prompt_states, conv_tails, resp_prompt, resp_lengths, rewards, upstream,
    conv_weight, conv_bias, dt_bias, a_log, d_skip, norm_gain,
):
    devices = lax.axis_size("dp") * lax.axis_size("fsdp")
    n_dp, n_fsdp = lax.axis_size("dp"), lax.axis_size("fsdp")
    dp = lax.axis_index("dp")
    holder = lax.axis_index(AXES)
    exchange = functools.partial(
        lax.all_to_all, axis_name=AXES, split_axis=0, concat_axis=0, tiled=True
    )

    weights = cat(
        [conv_weight.reshape(-1), conv_bias, dt_bias, a_log, d_skip, norm_gain], 0
    )
    count = weights.shape[0]
    weights = jnp.pad(weights, (0, 2048 - count))
    quarter = lax.dynamic_slice_in_dim(weights, dp * 512, 512)
    parts = three(quarter)
    quarter = cat(parts[:2], 0)
    onehot = resp_prompt[:, None] == jnp.arange(PROMPTS, dtype=jnp.int32)[None, :]
    tails_sent = jnp.dot(
        onehot.astype(BF16), conv_tails.reshape(PROMPTS, 240), preferred_element_type=F32
    ).astype(BF16)
    lengths_f = jnp.broadcast_to(resp_lengths.astype(BF16), (devices, DOCS))
    sent = cat(
        [
            tails_sent.reshape(devices, 960),
            lengths_f,
            jnp.broadcast_to(jnp.pad(parts[2][64:80], (0, 44))[None], (devices, 60)),
            jnp.broadcast_to(quarter[None], (devices, 1024)),
        ],
        1,
    )
    got = exchange(sent.reshape(devices, 16, 128)).reshape(devices, 2048)
    states = pl.pallas_call(
        gather_kernel,
        grid_spec=pltpu.PrefetchScalarGridSpec(
            num_scalar_prefetch=1,
            grid=(devices * DOCS // 32,),
            in_specs=[whole((PROMPTS, P_SIZE, N))],
            out_specs=lead(32, P_SIZE, N),
        ),
        out_shape=shape((devices * DOCS, P_SIZE, N), BF16),
        compiler_params=pltpu.CompilerParams(vmem_limit_bytes=56 * 1024 * 1024),
        cost_estimate=pl.CostEstimate(flops=0, bytes_accessed=16 * 10**6, transcendentals=0),
        name="gather_states",
    )(resp_prompt, prompt_states.reshape(PROMPTS, P_SIZE, N))
    states = exchange(states.reshape(devices, DOCS, P_SIZE, N))

    lengths, got = lax.optimization_barrier((resp_lengths[0], got))
    tails = got[:, :960].reshape(devices, 12, 80).transpose(1, 0, 2).reshape(12, CONV)
    tails = jnp.pad(tails, ((0, 4), (0, 0)))
    all_lengths = got[:, 960:964].astype(jnp.int32)
    third = jnp.pad(got[:, 964:980].astype(F32), ((0, 0), (64, 432)))
    full = third + got[:, 1536:].astype(F32) + got[:, 1024:1536].astype(F32)
    full = full.reshape(n_dp, n_fsdp, 512).transpose(1, 0, 2).reshape(n_fsdp, 2048)
    conv_w = full[:, :1280].reshape(n_fsdp, 4, 320).transpose(1, 0, 2).reshape(4, CONV)
    conv_b = full[:, 1280:1600].reshape(1, CONV)
    bias_dt = full[:, 1600:1604].reshape(1, H)
    rate = jnp.exp(full[:, 1604:1608].reshape(1, H))
    skip = full[:, 1608:1612].reshape(1, H)
    gain = full[:, 1612:1868].reshape(1, DI)

    places = jnp.arange(T, dtype=jnp.int32)
    ends = jnp.cumsum(lengths)
    starts = ends - lengths
    member = (places[:, None] >= starts[None, :]) & (places[:, None] < ends[None, :])
    start = jnp.sum(jnp.where(member, starts[None, :], 0), axis=1)
    offset = (places - start)[:, None]
    causal = ((start[:, None] == start[None, :]) & (places[:, None] >= places[None, :])).astype(F32)
    member_f = member.astype(F32)
    lag = jnp.arange(1, 4, dtype=jnp.int32)[:, None, None, None]
    row = jnp.arange(3, dtype=jnp.int32)[None, None, None, :]
    sel = member[None, :, :, None] & (offset[None, :, :, None] - lag + 3 == row)
    sel = jnp.pad(sel.reshape(3 * T, 12).astype(BF16), ((0, 0), (0, 4)))
    sel_rows = sel.reshape(3, T, 16).transpose(0, 2, 1).reshape(48, T)
    by_doc = resp_prompt.reshape(devices, DOCS).T.reshape(1, -1)
    members = (jnp.arange(PROMPTS, dtype=jnp.int32)[:, None] == by_doc).astype(BF16)
    all_ends = jnp.cumsum(all_lengths, axis=1)
    all_starts = all_ends - all_lengths
    mask_rows = (
        (places[None, None, :] >= all_starts[:, :, None])
        & (places[None, None, :] < all_ends[:, :, None])
    ).astype(F32)
    advantage = advantages(rewards, resp_prompt, PROMPTS)
    doc_weight = lax.dynamic_slice_in_dim(advantage, holder * DOCS, DOCS) * (
        T / (DOCS * lengths.astype(F32))
    )
    tokw = jnp.sum(jnp.where(member, doc_weight[None, :], 0.0), axis=1)[:, None]

    raw_step = dt_raw + bias_dt
    step = jax.nn.softplus(raw_step)
    decay = -step * rate
    rel = jnp.dot(causal, decay, precision=lax.Precision.HIGHEST)
    step_t = step.T
    rel_g = rel.reshape(T, G, HG).transpose(1, 0, 2)
    skip_wide = jnp.repeat(skip, P_SIZE, axis=1)

    groups = classes(devices)
    order = jnp.asarray(groups, jnp.int32)[color(holder) ^ jnp.arange(4, dtype=jnp.int32)]
    sig_t = jax.nn.sigmoid(raw_step).T
    rate_t, skip_t = jnp.broadcast_to(rate.T, (H, 128)), jnp.broadcast_to(skip.T, (H, 128))
    tokw = jnp.broadcast_to(tokw, (T, 128))
    member_f = jnp.pad(member_f, ((0, 0), (0, 128 - DOCS)))
    (offset, sel, sel_rows, causal, member_f, members, mask_rows, tokw, order, rate_t, skip_t, sig_t, step_t,
     conv_b) = lax.optimization_barrier(
        (offset, sel, sel_rows, causal, member_f, members, mask_rows, tokw, order, rate_t, skip_t, sig_t,
         step_t, conv_b)
    )

    conv_specs = [cols(T, GC), cols(T, N, 64), cols(T, N, 72)]
    tail_specs = [cols(16, GC), cols(16, N, 64), cols(16, N, 72)]
    tap_specs = [cols(4, GC), cols(4, N, 64), cols(4, N, 72)]
    bias_specs = [cols(1, GC), cols(1, N, 64), cols(1, N, 72)]
    x, b, c, spx, spb, spc, mixed0, lw, exr, cq, sc, scores = call(
        local_kernel,
        (G,),
        conv_specs + tail_specs + tap_specs + bias_specs
        + [whole((T, 1)), whole((3 * T, 16)), whole((T, T)), lead(1, T, HG), lead(HG, T), lead(HG, T),
           cols(1, GC)],
        [cols(T, GC), cols(T, N), cols(T, N), cols(T, GC), cols(T, N), cols(T, N), cols(T, GC),
         lead(HG, T, T), cols(T, GC), lead(4, T, N), lead(1, 1, T), lead(1, T, T)],
        [shape((T, DI)), shape((T, G * N)), shape((T, G * N)), shape((T, DI)), shape((T, G * N)),
         shape((T, G * N)), shape((T, DI)), shape((H, T, T)), shape((T, DI)),
         shape((4 * G, T, N), jnp.int16), shape((G, 1, T)), shape((G, T, T))],
        "local_forward", 0, 95 * 10**6,
    )(xbc, xbc, xbc, tails, tails, tails, conv_w, conv_w, conv_w, conv_b, conv_b, conv_b,
      offset, sel, causal, rel_g, rel.T, step_t, skip_wide)

    states, cq = lax.optimization_barrier((states, cq))
    near = [lax.all_to_all(cq, AXES, 0, 0, axis_index_groups=groups, tiled=True)]
    grad_z, dm, q, d_gain, rs = call(
        norm_kernel,
        (4,),
        [lead(32, DOCS, P_SIZE, N), cols(T, 2 * N), cols(T, GS), cols(T, GS), cols(T, GS), cols(T, GS),
         cols(1, GS), whole((T, 128)), whole((T, 128)), lead(2, 1, T)],
        [cols(T, GS), cols(T, GS), lead(32, Q_ROWS, T), cols(8, GS), lead(32, T)],
        [shape((T, DI), BF16), shape((T, DI)), shape((H, Q_ROWS, T), jnp.int16),
         shape((8, DI)), shape((H, T))],
        "norm_both_ways", 0, 52 * 10**6,
        [pltpu.VMEM((T, GS), F32)],
    )(states, c, mixed0, exr, zgate, upstream, gain, tokw, member_f, sc)
    q, dm, near[0] = lax.optimization_barrier((q, dm, near[0]))
    for bit in (1, 2, 8):
        near.append(lax.ppermute(near[0], AXES, [(d, d ^ bit) for d in range(devices)]))
    got_q = exchange(q)

    gx, gb, gc, grad_dt, back = call(
        back_kernel,
        (G,),
        [lead(HG, DOCS, P_SIZE, N), cols(T, GC), cols(T, GC), lead(HG, T, T), lead(1, T, T),
         cols(T, GC), cols(T, N), cols(T, N), cols(T, GC), cols(T, N), cols(T, N)]
        + conv_specs + tail_specs + tap_specs
        + [whole((T, 1)), whole((48, T)), whole((T, 128)), cols(1, GC), whole((T, T)), lead(HG, T),
           lead(HG, T), lead(HG, T), lead(HG, 128), lead(HG, 128), whole((8, DI))],
        [cols(T, GC), cols(T, N), cols(T, N), lead(HG, T), whole((devices, 24, 128))],
        [shape((T, DI), BF16), shape((T, G * N), BF16), shape((T, G * N), BF16), shape((H, T)),
         shape((devices, 24, 128))],
        "local_backward", 0, 133 * 10**6,
        [pltpu.VMEM((24, AHEAD + CONV + 128), F32), pltpu.VMEM((H, 128), F32)],
    )(states, dm, exr, lw, scores, x, b, c, spx, spb, spc, xbc, xbc, xbc, tails, tails, tails,
      conv_w, conv_w, conv_w, offset, sel_rows, member_f, skip_wide, causal, rs, step_t,
      sig_t, rate_t, skip_t, d_gain)

    gx, gb, gc, grad_dt, back, got_q = lax.optimization_barrier((gx, gb, gc, grad_dt, back, got_q))
    grad_x = cat([gx, gb, gc], 1)
    back = exchange(back)

    def add_states(kinds, *before):
        return pl.pallas_call(
            functools.partial(state_kernel, kinds),
            grid_spec=pltpu.PrefetchScalarGridSpec(
                num_scalar_prefetch=2,
                grid=(1,),
                in_specs=[whole((devices, Q_ROWS, T))] + [whole((devices // 4, T, N))] * len(kinds)
                + [whole((devices, DOCS, T))] + [whole((PROMPTS, P_SIZE, N))] * len(before),
                out_specs=whole((PROMPTS, P_SIZE, N)),
            ),
            out_shape=shape((PROMPTS, P_SIZE, N)),
            compiler_params=pltpu.CompilerParams(vmem_limit_bytes=56 * 1024 * 1024),
            cost_estimate=pl.CostEstimate(
                flops=0, bytes_accessed=15 * 10**6 * len(kinds), transcendentals=0
            ),
            name="state_gradients_%d" % len(kinds),
        )(order, resp_prompt, got_q, *[near[k] for k in kinds], mask_rows, *before)

    grad_states = add_states((0,))
    grad_states = add_states((1, 2, 3), grad_states)

    share = CONV // n_fsdp
    grad_tails, grad_w, grad_b, grad_gain, *heads = call(
        finish_kernel,
        (1,),
        [whole((devices, 24, 128)), whole((PROMPTS, devices * DOCS))],
        [whole((3, PROMPTS, 80)), whole((4, share)), whole((share,)), whole((1, 256))] + [whole((1, 4))] * 3,
        [shape((3, PROMPTS, 80)), shape((4, share)), shape((share,)), shape((1, 256))] + [shape((1, 4))] * 3,
        "finish", 0, 10 * 10**6,
    )(back, members)
    return (
        grad_x,
        grad_z,
        grad_dt.T,
        grad_states.reshape(PROMPTS, 1, P_SIZE, N),
        grad_tails.transpose(1, 0, 2),
        grad_w,
        grad_b,
        heads[0].reshape(4),
        heads[1].reshape(4),
        heads[2].reshape(4),
        grad_gain.reshape(256),
    )


def solution(mesh):
    whole_axis = P(AXES, None)
    weight = P("fsdp")
    return jax.shard_map(
        shards,
        mesh=mesh,
        in_specs=(
            whole_axis, whole_axis, whole_axis, P(None, AXES, None, None), P(None, None, AXES),
            P(), whole_axis, P(), whole_axis, P(None, "fsdp"), weight, weight, weight, weight, weight,
        ),
        out_specs=(
            whole_axis, whole_axis, whole_axis, P(None, AXES, None, None), P(None, None, AXES),
            P(None, "fsdp"), weight, weight, weight, weight, weight,
        ),
        check_vma=False,
    )
```
